32 devices in a mesh: grp: 1, pool: 16 (over z, y, x), samp: 2 (over core).
Axes of the slice: x: 2, y: 2, z: 4, core: 2. Of those that a mesh axis runs over, the one named last changes fastest.
Arguments:
- samples: bfloat16 [2, 1024, 1024], P(('grp', 'samp'), 'pool'), may hold values from -11 to 11
- pool: bfloat16 [16384, 1024], P(('grp', 'pool')), may hold values from -11 to 11
- tile_list: int32 [2, 16, 4, 2], P(('grp', 'samp'), 'pool'), may hold values from 0 to 1, as said below
- tile_count: int32 [2, 16], P(('grp', 'samp'), 'pool'), may hold values from 1 to 4, as said below
Outputs:
- sample_potential: float32 [2, 1024], P(('grp', 'samp'), 'pool')
- pool_potential: float32 [16384], P(('grp', 'pool'))
The draws below stay inside these ranges and needn't reach their ends.
Inputs may be any that keep to these rules, and one draw needn't show every extreme that they name: `tile_list`: entry [h, p, k] is a pair (sample tile of half h, 0 to 1; one of the 2 tiles of pool device p). The 4 pairs of one (h, p) are distinct, and among the counted pairs every sample tile and every pool tile appears at least once. The first tile_count[h, p] pairs of tile_list[h, p] count; 4 on at least one (h, p).
All inputs are finite; a program needn't handle non-finite values.
Results may differ from the reference program's by a relative error of at most 0.0003.
Values may be sent and summed in bfloat16 or wider, within the bound.
No kernel may reach another device: no remote copies, remote signals or barrier semaphores. Data moves between devices by JAX's collectives and lax.ppermute only.
A program may use at most 64 MiB of HBM per device.

```python
import math
import jax
import jax.numpy as jnp
from jax import lax

D = 1024
TILE = 512
PT = 2
CAP = 4
ITERS = 3
SAMP_HALF = 1024
ST = 2
NS = 2048
NP = 16384
N_POOL = 16
N_SAMP = 2


def draw_samples(key, part):
    key = jax.random.fold_in(key, 21)
    values = jnp.clip(jax.random.normal(key, (N_SAMP, SAMP_HALF, D), jnp.float32), -6.0, 6.0)
    return values.astype(jnp.bfloat16)


def draw_pool(key, part):
    key = jax.random.fold_in(key, 22)
    values = jnp.clip(jax.random.normal(key, (NP, D), jnp.float32), -6.0, 6.0)
    return values.astype(jnp.bfloat16)


def draw_tile_list(key, part):
    key = jax.random.fold_in(key, 11)
    pair_total = ST * PT
    halves = jnp.arange(N_SAMP, dtype=jnp.int32)[:, None]
    owners = jnp.arange(N_POOL, dtype=jnp.int32)[None, :]
    first_pair = owners % ST * PT + (owners + halves) % PT
    labels = jnp.arange(pair_total, dtype=jnp.int32)
    scores = jax.random.randint(key, (N_SAMP, N_POOL, pair_total), 0, 1 << 20, jnp.int32) * pair_total + labels
    scores = jnp.where(labels == first_pair[:, :, None], -1, scores)
    order = jnp.argsort(scores, axis=-1, stable=True)[:, :, :CAP].astype(jnp.int32)
    return jnp.stack([order // PT, order % PT], axis=-1).astype(jnp.int32)


def draw_tile_count(key, part):
    key = jax.random.fold_in(key, 12)
    draws = jax.random.randint(key, (N_SAMP * N_POOL,), 0, 4, jnp.int32)
    counts = jnp.where(draws < 2, 1, jnp.where(draws < 3, min(2, CAP), CAP)).astype(jnp.int32)
    busiest = jax.random.randint(jax.random.fold_in(key, 1), (), 0, N_SAMP * N_POOL, jnp.int32)
    mate = busiest // N_POOL * N_POOL + (busiest % N_POOL + N_POOL // 2) % N_POOL
    counts = counts.at[busiest].set(CAP)
    counts = counts.at[mate].set(1)
    return counts.reshape(N_SAMP, N_POOL).astype(jnp.int32)


def setup_inputs(seed: int = 0, part: int = 0) -> dict:
    splits = jax.random.split(jax.random.key(seed), 5)
    own_keys = jax.random.split(jax.random.fold_in(splits[4], part), 5)
    return {
        "samples": draw_samples(jax.random.fold_in(jax.random.fold_in(splits[4], part), 71), part),
        "pool": draw_pool(jax.random.fold_in(jax.random.fold_in(splits[4], part), 71), part),
        "tile_list": draw_tile_list(jax.random.fold_in(jax.random.fold_in(splits[4], part), 71), part),
        "tile_count": draw_tile_count(jax.random.fold_in(jax.random.fold_in(splits[4], part), 71), part),
    }


EPS = 0.02
NEG = -1.0e30


def distance_tile(rows, columns):
    dots = jnp.einsum("id,jd->ij", rows, columns, preferred_element_type=jnp.float32)
    row_norm = jnp.sum(jnp.square(rows.astype(jnp.float32)), axis=1)
    column_norm = jnp.sum(jnp.square(columns.astype(jnp.float32)), axis=1)
    return (row_norm[:, None] + column_norm[None, :] - 2.0 * dots) / D


def soft_min(shifted, axis, valid, target, groups, log_mass):
    scores = shifted / EPS
    local = jnp.max(scores, axis=axis)
    local = jnp.where(valid[:, None], local, NEG)
    peak = jnp.full((groups, TILE), NEG, jnp.float32).at[target].max(local)
    spot = jnp.expand_dims(peak[target], axis)
    terms = jnp.sum(jnp.exp(scores - spot), axis=axis)
    terms = jnp.where(valid[:, None], terms, 0.0)
    total = jnp.zeros((groups, TILE), jnp.float32).at[target].add(terms)
    return EPS * (log_mass - peak - jnp.log(total))


def reference(samples, pool, tile_list, tile_count):
    slots = N_SAMP * N_POOL * CAP
    index = jnp.arange(slots, dtype=jnp.int32)
    device = index // CAP
    half = device // N_POOL
    owner = device % N_POOL
    flat = tile_list.reshape(slots, 2).astype(jnp.int32)
    valid = (index % CAP) < tile_count.reshape(-1)[device]
    sample_tile = (half * ST + flat[:, 0]).astype(jnp.int32)
    pool_tile = (owner * PT + flat[:, 1]).astype(jnp.int32)
    sample_blocks = samples.reshape(N_SAMP * ST, TILE, D)
    pool_blocks = pool.reshape(N_POOL * PT, TILE, D)
    costs = lax.map(lambda k: distance_tile(sample_blocks[sample_tile[k]], pool_blocks[pool_tile[k]]), index)
    pool_potential = jnp.zeros((N_POOL * PT, TILE), jnp.float32)
    sample_potential = jnp.zeros((N_SAMP * ST, TILE), jnp.float32)
    for step in range(ITERS):
        sample_potential = soft_min(pool_potential[pool_tile][:, None, :] - costs, 2, valid, sample_tile, N_SAMP * ST, -math.log(NS))
        pool_potential = soft_min(sample_potential[sample_tile][:, :, None] - costs, 1, valid, pool_tile, N_POOL * PT, -math.log(NP))
    return sample_potential.reshape(N_SAMP, SAMP_HALF), pool_potential.reshape(NP)
```

```python
import functools
import math

import jax
import jax.numpy as jnp
from jax import lax
from jax.experimental import pallas as pl
from jax.experimental.pallas import tpu as pltpu
from jax.sharding import PartitionSpec as P

TILE = 512
CAP = 4
ITERS = 3


EPS = 0.02
NEG = -1e30
LN2 = math.log(2.0)
VMEM_LIMIT = 32 * 1024 * 1024


def log2_sum(values):
    peak = functools.reduce(jnp.maximum, values)
    total = functools.reduce(jnp.add, [jnp.exp2(v - peak) for v in values])
    return peak + jnp.log(total) * (1.0 / LN2)


def score_kernel(rel, scale, own_rows, me_ref, list_ref, count_ref, *refs):
    pool_ref, out_ref = refs[-2:]
    me = me_ref[0]
    tiles = pool_ref.shape[0] // TILE
    first = 0
    for rows_ref in refs[:-2]:
        dots = lax.dot_general(
            rows_ref[...],
            pool_ref[...],
            (((1,), (1,)), ((), ())),
            preferred_element_type=jnp.float32,
        )
        for part in range(rows_ref.shape[0] // own_rows):
            tile = lax.div((me ^ rel[first + part]) * own_rows, TILE)
            low = (first + part) * own_rows
            for u in range(tiles):
                counted = jnp.int32(0)
                for k in range(CAP):
                    hit = (k < count_ref[0]) & (list_ref[k, 0] == tile) & (list_ref[k, 1] == u)
                    counted += jnp.where(hit, 1, 0)
                offset = jnp.where(counted > 0, 0.0, NEG)
                block = dots[part * own_rows : (part + 1) * own_rows, u * TILE : (u + 1) * TILE]
                out_ref[low : low + own_rows, u * TILE : (u + 1) * TILE] = block * scale + offset
        first += rows_ref.shape[0] // own_rows


def diagonal(size):
    rows = lax.broadcasted_iota(jnp.int32, (size, size), 0)
    return rows == lax.broadcasted_iota(jnp.int32, (size, size), 1)


def row_kernel(rels, own_rows, me_ref, shift_ref, *refs):
    out_ref = refs[-1]
    me = me_ref[0]
    shift = shift_ref[...]
    eye = diagonal(own_rows)
    for ref, rel in zip(refs[:-1], rels):
        for part, source in enumerate(rel):
            block = ref[part * own_rows : (part + 1) * own_rows, :] + shift
            peak = jnp.max(block, axis=1, keepdims=True)
            total = jnp.sum(jnp.exp2(block - peak), axis=1, keepdims=True)
            column = peak + jnp.log(total) * (1.0 / LN2)
            row = jnp.sum(jnp.where(eye, column, 0.0), axis=0, keepdims=True)
            out_ref[pl.ds(me ^ source, 1), :] = row


def column_kernel(rels, own_rows, me_ref, shift_ref, *refs):
    out_ref = refs[-1]
    me = me_ref[0]
    eye = diagonal(own_rows)
    columns = []
    peak = None
    for ref, rel in zip(refs[:-1], rels):
        for part, source in enumerate(rel):
            row = shift_ref[pl.ds(me ^ source, 1), :]
            column = jnp.sum(jnp.where(eye, row, 0.0), axis=1, keepdims=True)
            columns.append(column)
            block = ref[part * own_rows : (part + 1) * own_rows, :] + column
            high = jnp.max(block.reshape(own_rows // 8, 8, block.shape[1]), axis=0)
            peak = high if peak is None else jnp.maximum(peak, high)
    peak = jnp.max(peak, axis=0, keepdims=True)
    total = jnp.zeros((8, peak.shape[1]), jnp.float32)
    for ref, rel in zip(refs[:-1], rels):
        for part, source in enumerate(rel):
            column = columns.pop(0)
            block = ref[part * own_rows : (part + 1) * own_rows, :] + (column - peak)
            total += jnp.sum(jnp.exp2(block).reshape(own_rows // 8, 8, block.shape[1]), axis=0)
    total = jnp.sum(total, axis=0, keepdims=True)
    out_ref[...] = peak + jnp.log(total) * (1.0 / LN2)


def call(kernel, out_shape, scalars, arrays, flops, name):
    smem = pl.BlockSpec(memory_space=pltpu.SMEM)
    vmem = pl.BlockSpec(memory_space=pltpu.VMEM)
    moved = sum(a.size * a.dtype.itemsize for a in arrays) + 4 * math.prod(out_shape)
    return pl.pallas_call(
        kernel,
        out_shape=jax.ShapeDtypeStruct(out_shape, jnp.float32),
        in_specs=[smem] * len(scalars) + [vmem] * len(arrays),
        out_specs=vmem,
        compiler_params=pltpu.CompilerParams(vmem_limit_bytes=VMEM_LIMIT),
        cost_estimate=pl.CostEstimate(flops=flops, bytes_accessed=moved, transcendentals=0),
        name=name,
    )(*scalars, *arrays)


def body(samples, pool, tile_list, tile_count):
    own_rows, width = samples.shape[1:]
    size = lax.axis_size("pool")
    half_rows = own_rows * size
    pool_rows = pool.shape[0]
    unit = EPS * LN2
    log_a = -math.log2(half_rows * lax.axis_size("samp"))
    log_b = -math.log2(pool_rows * size)
    me = lax.axis_index("pool").astype(jnp.int32).reshape(1)
    scalars = [me, tile_list.reshape(CAP, 2), tile_count.reshape(1)]
    own = samples.reshape(own_rows, width)

    def swap(value, mask):
        return lax.ppermute(value, "pool", [(i, i ^ mask) for i in range(size)])

    def score(pieces, rels):
        rel = sum(rels, ())
        shape = (len(rel) * own_rows, pool_rows)
        flops = 2 * shape[0] * pool_rows * width
        kernel = functools.partial(score_kernel, rel, 2.0 / (width * unit), own_rows)
        return call(kernel, shape, scalars, pieces + [pool], flops, "score"), rel

    outer = tuple(range(0, size, 4))
    plane = jnp.concatenate([own] + [swap(own, m) for m in outer[1:]], axis=0)
    half = plane.shape[0] // 2
    first, second = outer[: size // 8], outer[size // 8 :]
    by_x = swap(plane, 1)
    by_y = swap(plane, 2)
    low = swap(by_x[:half], 2)
    high = swap(by_y[half:], 1)
    parts = [
        score([plane], [outer]),
        score([by_x, by_y], [tuple(m ^ 1 for m in outer), tuple(m ^ 2 for m in outer)]),
        score([low, high], [tuple(m ^ 3 for m in first), tuple(m ^ 3 for m in second)]),
    ]
    scores = [p[0] for p in parts]
    rels = [p[1] for p in parts]

    own_norm = jnp.sum(jnp.square(own.astype(jnp.float32)), axis=1) / width
    pool_norm = jnp.sum(jnp.square(pool.astype(jnp.float32)), axis=1) / width
    shift = pool_norm.reshape(1, pool_rows) * (-1.0 / unit)
    flops = 8 * half_rows * pool_rows
    for _ in range(ITERS):
        kernel = functools.partial(row_kernel, rels, own_rows)
        value = call(kernel, (size, own_rows), [me], [shift] + scores, flops, "rows")
        step = 1
        while step < size:
            masks = [m * step for m in range(1, min(4, size // step))]
            value = log2_sum([value] + [swap(value, m) for m in masks])
            step *= 4
        sample_shift = log_a - value
        kernel = functools.partial(column_kernel, rels, own_rows)
        value = call(kernel, (1, pool_rows), [me], [sample_shift] + scores, flops, "columns")
        pairs = [(i, i ^ 1) for i in range(2)]
        shift = log_b - log2_sum([value, lax.ppermute(value, "samp", pairs)])
    mine = lax.dynamic_slice_in_dim(sample_shift, me[0], 1, 0)
    return mine * unit + own_norm[None, :], shift.reshape(pool_rows) * unit + pool_norm


def solution(mesh):
    placed = (
        P(("grp", "samp"), "pool", None),
        P(("grp", "pool"), None),
        P(("grp", "samp"), "pool", None, None),
        P(("grp", "samp"), "pool"),
    )
    return jax.shard_map(
        body,
        mesh=mesh,
        in_specs=placed,
        out_specs=(P(("grp", "samp"), "pool"), P(("grp", "pool"))),
        check_vma=False,
    )
```

```python
import functools
import math

import jax
import jax.numpy as jnp
from jax import lax
from jax.experimental import pallas as pl
from jax.experimental.pallas import tpu as pltpu
from jax.sharding import PartitionSpec as P

TILE = 512
CAP = 4
ITERS = 3


EPS = 0.02
NEG = -1e30
LN2 = math.log(2.0)
LANES = 128
VMEM_LIMIT = 32 * 1024 * 1024


def log2_sum(values):
    peak = functools.reduce(jnp.maximum, values)
    total = functools.reduce(jnp.add, [jnp.exp2(v - peak) for v in values])
    return peak + jnp.log(total) * (1.0 / LN2)


def score_kernel(rel, scale, own_rows, me_ref, list_ref, count_ref, *refs):
    pool_ref, out_ref = refs[-2:]
    me = me_ref[0]
    tiles = pool_ref.shape[0] // TILE
    first = 0
    for rows_ref in refs[:-2]:
        dots = lax.dot_general(
            rows_ref[...],
            pool_ref[...],
            (((1,), (1,)), ((), ())),
            preferred_element_type=jnp.float32,
        )
        for part in range(rows_ref.shape[0] // own_rows):
            tile = lax.div((me ^ rel[first + part]) * own_rows, TILE)
            low = (first + part) * own_rows
            for u in range(tiles):
                counted = jnp.int32(0)
                for k in range(CAP):
                    hit = (k < count_ref[0]) & (list_ref[k, 0] == tile) & (list_ref[k, 1] == u)
                    counted += jnp.where(hit, 1, 0)
                offset = jnp.where(counted > 0, 0.0, NEG)
                block = dots[part * own_rows : (part + 1) * own_rows, u * TILE : (u + 1) * TILE]
                out_ref[low : low + own_rows, u * TILE : (u + 1) * TILE] = block * scale + offset
        first += rows_ref.shape[0] // own_rows


def diagonal(size):
    rows = lax.broadcasted_iota(jnp.int32, (size, size), 0)
    return rows == lax.broadcasted_iota(jnp.int32, (size, size), 1)


def row_kernel(rels, own_rows, me_ref, shift_ref, *refs):
    out_ref, held_ref = refs[-2:]
    me = me_ref[0]
    shift = shift_ref[...]
    eye = diagonal(own_rows)
    for ref, rel in zip(refs[:-2], rels):
        for part, source in enumerate(rel):
            block = ref[part * own_rows : (part + 1) * own_rows, :] + shift
            peak = jnp.max(block, axis=1, keepdims=True)
            total = jnp.sum(jnp.exp2(block - peak), axis=1, keepdims=True)
            column = peak + jnp.log(total) * (1.0 / LN2)
            row = jnp.sum(jnp.where(eye, column, 0.0), axis=0, keepdims=True)
            held_ref[pl.ds(me ^ source, 1), :] = row
    across = out_ref.shape[2] // own_rows
    for line in range(out_ref.shape[1]):
        sources = [held_ref[line * across + k : line * across + k + 1, :] for k in range(across)]
        wide = jnp.concatenate(sources, axis=1)
        out_ref[:, line, :] = jnp.broadcast_to(wide, (out_ref.shape[0], out_ref.shape[2]))


def column_kernel(rels, own_rows, log_a, me_ref, value_ref, *refs):
    out_ref, held_ref = refs[-2:]
    me = me_ref[0]
    shift = log_a - log2_sum([value_ref[k] for k in range(value_ref.shape[0])])
    across = shift.shape[1] // own_rows
    for source in range(held_ref.shape[0]):
        line, place = source // across, source % across
        held_ref[source : source + 1, :] = shift[
            line : line + 1, place * own_rows : (place + 1) * own_rows
        ]
    eye = diagonal(own_rows)
    columns = []
    peak = None
    for ref, rel in zip(refs[:-2], rels):
        for part, source in enumerate(rel):
            row = held_ref[pl.ds(me ^ source, 1), :]
            column = jnp.sum(jnp.where(eye, row, 0.0), axis=1, keepdims=True)
            columns.append(column)
            block = ref[part * own_rows : (part + 1) * own_rows, :] + column
            high = jnp.max(block.reshape(own_rows // 8, 8, block.shape[1]), axis=0)
            peak = high if peak is None else jnp.maximum(peak, high)
    peak = jnp.max(peak, axis=0, keepdims=True)
    total = jnp.zeros((8, peak.shape[1]), jnp.float32)
    for ref, rel in zip(refs[:-2], rels):
        for part, source in enumerate(rel):
            column = columns.pop(0)
            block = ref[part * own_rows : (part + 1) * own_rows, :] + (column - peak)
            total += jnp.sum(jnp.exp2(block).reshape(own_rows // 8, 8, block.shape[1]), axis=0)
    total = jnp.sum(total, axis=0, keepdims=True)
    out_ref[...] = peak + jnp.log(total) * (1.0 / LN2)


def call(kernel, shapes, scratch, scalars, arrays, flops, name):
    smem = pl.BlockSpec(memory_space=pltpu.SMEM)
    vmem = pl.BlockSpec(memory_space=pltpu.VMEM)
    moved = sum(a.size * a.dtype.itemsize for a in arrays) + 4 * sum(map(math.prod, shapes))
    return pl.pallas_call(
        kernel,
        out_shape=[jax.ShapeDtypeStruct(s, jnp.float32) for s in shapes],
        in_specs=[smem] * len(scalars) + [vmem] * len(arrays),
        out_specs=[vmem] * len(shapes),
        scratch_shapes=scratch,
        compiler_params=pltpu.CompilerParams(vmem_limit_bytes=VMEM_LIMIT),
        cost_estimate=pl.CostEstimate(flops=flops, bytes_accessed=moved, transcendentals=0),
        name=name,
    )(*scalars, *arrays)


def body(samples, pool, tile_list, tile_count):
    own_rows, width = samples.shape[1:]
    size = lax.axis_size("pool")
    half_rows = own_rows * size
    pool_rows = pool.shape[0]
    unit = EPS * LN2
    log_a = -math.log2(half_rows * lax.axis_size("samp"))
    log_b = -math.log2(pool_rows * size)
    me = lax.axis_index("pool").astype(jnp.int32).reshape(1)
    scalars = [me, tile_list.reshape(CAP, 2), tile_count.reshape(1)]
    own = samples.reshape(own_rows, width)

    def swap(value, mask):
        return lax.ppermute(value, "pool", [(i, i ^ mask) for i in range(size)])

    def score(pieces, rels):
        rel = sum(rels, ())
        shape = (len(rel) * own_rows, pool_rows)
        flops = 2 * shape[0] * pool_rows * width
        kernel = functools.partial(score_kernel, rel, 2.0 / (width * unit), own_rows)
        return call(kernel, [shape], [], scalars, pieces + [pool], flops, "score")[0], rel

    outer = tuple(range(0, size, 4))
    plane = jnp.concatenate([own] + [swap(own, m) for m in outer[1:]], axis=0)
    half = plane.shape[0] // 2
    first, second = outer[: size // 8], outer[size // 8 :]
    by_x = swap(plane, 1)
    by_y = swap(plane, 2)
    center = score([plane], [outer])
    by_x, by_y, center_score = lax.optimization_barrier((by_x, by_y, center[0]))
    low = swap(by_x[:half], 2)
    high = swap(by_y[half:], 1)
    sides = score([by_x, by_y], [tuple(m ^ 1 for m in outer), tuple(m ^ 2 for m in outer)])
    low, high, sides_score = lax.optimization_barrier((low, high, sides[0]))
    corner = score([low, high], [tuple(m ^ 3 for m in first), tuple(m ^ 3 for m in second)])
    parts = [(center_score, center[1]), (sides_score, sides[1]), corner]
    scores = [p[0] for p in parts]
    rels = [p[1] for p in parts]

    own_norm = jnp.sum(jnp.square(own.astype(jnp.float32)), axis=1) / width
    pool_norm = jnp.sum(jnp.square(pool.astype(jnp.float32)), axis=1) / width
    shift = pool_norm.reshape(1, pool_rows) * (-1.0 / unit)
    lines = half_rows // LANES
    held = [pltpu.VMEM((size, own_rows), jnp.float32)]
    flops = 8 * half_rows * pool_rows
    for _ in range(ITERS):
        kernel = functools.partial(row_kernel, rels, own_rows)
        (value,) = call(
            kernel, [(size, lines, LANES)], held, [me], [shift] + scores, flops, "rows"
        )
        value = lax.all_to_all(value, "pool", 0, 0, tiled=True)
        kernel = functools.partial(column_kernel, rels, own_rows, log_a)
        value, potential = call(
            kernel,
            [(1, pool_rows), (size, own_rows)],
            [],
            [me],
            [value] + scores,
            flops,
            "columns",
        )
        pairs = [(i, i ^ 1) for i in range(2)]
        shift = log_b - log2_sum([value, lax.ppermute(value, "samp", pairs)])
    mine = lax.dynamic_slice_in_dim(potential, me[0], 1, 0)
    return mine * unit + own_norm[None, :], shift.reshape(pool_rows) * unit + pool_norm


def solution(mesh):
    placed = (
        P(("grp", "samp"), "pool", None),
        P(("grp", "pool"), None),
        P(("grp", "samp"), "pool", None, None),
        P(("grp", "samp"), "pool"),
    )
    return jax.shard_map(
        body,
        mesh=mesh,
        in_specs=placed,
        out_specs=(P(("grp", "samp"), "pool"), P(("grp", "pool"))),
        check_vma=False,
    )
```

```python
import functools
import math

import jax
import jax.numpy as jnp
from jax import lax
from jax.experimental import pallas as pl
from jax.experimental.pallas import tpu as pltpu
from jax.sharding import PartitionSpec as P

TILE = 512
CAP = 4
ITERS = 3


EPS = 0.02
NEG = -1e30
LN2 = math.log(2.0)
LANES = 128
VMEM_LIMIT = 20 * 1024 * 1024


def log2_sum(values):
    peak = functools.reduce(jnp.maximum, values)
    total = functools.reduce(jnp.add, [jnp.exp2(v - peak) for v in values])
    return peak + jnp.log(total) * (1.0 / LN2)


def diagonal(size):
    rows = lax.broadcasted_iota(jnp.int32, (size, size), 0)
    return rows == lax.broadcasted_iota(jnp.int32, (size, size), 1)


def row_sums(block):
    peak = jnp.max(block, axis=1, keepdims=True)
    total = jnp.sum(jnp.exp2(block - peak), axis=1, keepdims=True)
    column = peak + jnp.log(total) * (1.0 / LN2)
    return jnp.sum(jnp.where(diagonal(block.shape[0]), column, 0.0), axis=0, keepdims=True)


def copy_out(held_ref, out_ref):
    across = out_ref.shape[2] // held_ref.shape[1]
    for line in range(out_ref.shape[1]):
        sources = [held_ref[line * across + k : line * across + k + 1, :] for k in range(across)]
        wide = jnp.concatenate(sources, axis=1)
        out_ref[:, line, :] = jnp.broadcast_to(wide, (out_ref.shape[0], out_ref.shape[2]))


def score_kernel(pieces, blocks, own_rows, scale, me_ref, list_ref, count_ref, *refs):
    rows_refs = refs[:pieces]
    pool_ref, shift_ref, before_ref, score_ref, held_ref = refs[pieces : pieces + 5]
    me = me_ref[0]
    shift = shift_ref[...]
    tiles = pool_ref.shape[0] // TILE
    rows = rows_refs[0]
    if pieces > 1:
        rows = refs[-1]
        low = 0
        for ref in rows_refs:
            rows[low : low + ref.shape[0], :] = ref[...]
            low += ref.shape[0]
    dots = lax.dot_general(
        rows[...],
        pool_ref[...],
        (((1,), (1,)), ((), ())),
        preferred_element_type=jnp.float32,
    )
    held_ref[...] = before_ref[...]
    low = 0
    for source, first, count in blocks:
        owner = me ^ source
        tile = lax.div(owner * own_rows, TILE)
        parts = []
        for u in range(tiles):
            counted = jnp.int32(0)
            for k in range(CAP):
                hit = (k < count_ref[0]) & (list_ref[k, 0] == tile) & (list_ref[k, 1] == u)
                counted += jnp.where(hit, 1, 0)
            offset = jnp.where(counted > 0, 0.0, NEG)
            parts.append(dots[low : low + count, u * TILE : (u + 1) * TILE] * scale + offset)
        block = jnp.concatenate(parts, axis=1)
        score_ref[low : low + count, :] = block
        held_ref[pl.ds(owner, 1), first : first + count] = row_sums(block + shift)
        low += count


def last_score_kernel(pieces, blocks, own_rows, scale, *refs):
    inputs = pieces + 6
    score_ref, out_ref, held_ref = refs[inputs : inputs + 3]
    head = refs[:inputs] + (score_ref, held_ref)
    score_kernel(pieces, blocks, own_rows, scale, *head, *refs[inputs + 3 :])
    copy_out(held_ref, out_ref)


def row_kernel(parts, me_ref, shift_ref, *refs):
    out_ref, held_ref = refs[-2:]
    me = me_ref[0]
    shift = shift_ref[...]
    for ref, blocks in zip(refs[:-2], parts):
        low = 0
        for source, first, count in blocks:
            sums = row_sums(ref[low : low + count, :] + shift)
            held_ref[pl.ds(me ^ source, 1), first : first + count] = sums
            low += count
    copy_out(held_ref, out_ref)


def column_kernel(parts, log_a, me_ref, value_ref, *refs):
    out_ref, held_ref = refs[-2:]
    me = me_ref[0]
    shift = log_a - log2_sum([value_ref[k] for k in range(value_ref.shape[0])])
    own_rows = held_ref.shape[1]
    across = shift.shape[1] // own_rows
    for source in range(held_ref.shape[0]):
        line, place = source // across, source % across
        held_ref[source : source + 1, :] = shift[
            line : line + 1, place * own_rows : (place + 1) * own_rows
        ]
    columns = []
    peak = None
    for ref, blocks in zip(refs[:-2], parts):
        low = 0
        for source, first, count in blocks:
            row = held_ref[pl.ds(me ^ source, 1), first : first + count]
            column = jnp.sum(jnp.where(diagonal(count), row, 0.0), axis=1, keepdims=True)
            columns.append(column)
            block = ref[low : low + count, :] + column
            high = jnp.max(block.reshape(count // 8, 8, block.shape[1]), axis=0)
            peak = high if peak is None else jnp.maximum(peak, high)
            low += count
    peak = jnp.max(peak, axis=0, keepdims=True)
    total = jnp.zeros((8, peak.shape[1]), jnp.float32)
    for ref, blocks in zip(refs[:-2], parts):
        low = 0
        for source, first, count in blocks:
            block = ref[low : low + count, :] + (columns.pop(0) - peak)
            total += jnp.sum(jnp.exp2(block).reshape(count // 8, 8, block.shape[1]), axis=0)
            low += count
    total = jnp.sum(total, axis=0, keepdims=True)
    out_ref[...] = peak + jnp.log(total) * (1.0 / LN2)


def call(kernel, shapes, scratch, scalars, arrays, flops, name):
    smem = pl.BlockSpec(memory_space=pltpu.SMEM)
    vmem = pl.BlockSpec(memory_space=pltpu.VMEM)
    moved = sum(a.size * a.dtype.itemsize for a in arrays) + 4 * sum(map(math.prod, shapes))
    return pl.pallas_call(
        kernel,
        out_shape=[jax.ShapeDtypeStruct(s, jnp.float32) for s in shapes],
        in_specs=[smem] * len(scalars) + [vmem] * len(arrays),
        out_specs=[vmem] * len(shapes),
        scratch_shapes=scratch,
        compiler_params=pltpu.CompilerParams(vmem_limit_bytes=VMEM_LIMIT),
        cost_estimate=pl.CostEstimate(flops=flops, bytes_accessed=moved, transcendentals=0),
        name=name,
    )(*scalars, *arrays)


def body(samples, pool, tile_list, tile_count):
    own_rows, width = samples.shape[1:]
    size = lax.axis_size("pool")
    half_rows = own_rows * size
    pool_rows = pool.shape[0]
    unit = EPS * LN2
    log_a = -math.log2(half_rows * lax.axis_size("samp"))
    log_b = -math.log2(pool_rows * size)
    me = lax.axis_index("pool").astype(jnp.int32).reshape(1)
    own = samples.reshape(own_rows, width)

    def swap(value, mask):
        return lax.ppermute(value, "pool", [(i, i ^ mask) for i in range(size)])

    def score(pieces, blocks, before, last=False):
        count = sum(b[2] for b in blocks)
        shapes = [(count, pool_rows)] + [(size, lines, LANES)] * last + [(size, own_rows)]
        kernel = last_score_kernel if last else score_kernel
        return call(
            functools.partial(kernel, len(pieces), blocks, own_rows, 2.0 / (width * unit)),
            shapes,
            [pltpu.VMEM((count, width), samples.dtype)] * (len(pieces) > 1),
            [me, tile_list.reshape(CAP, 2), tile_count.reshape(1)],
            pieces + [pool, shift, before],
            2 * count * pool_rows * width,
            "score",
        )

    lines = half_rows // LANES
    own_norm = jnp.sum(jnp.square(own.astype(jnp.float32)), axis=1) / width
    pool_norm = jnp.sum(jnp.square(pool.astype(jnp.float32)), axis=1) / width
    shift = pool_norm.reshape(1, pool_rows) * (-1.0 / unit)
    near = (1, 2, 3)
    far = tuple(range(4, size, 4))
    cut = own_rows * 3 // 4
    rest = own_rows - cut
    top = own[:cut]
    by_far = [swap(top, m) for m in far]
    by_near = [swap(own, m) for m in near]
    blocks0 = [(m, 0, own_rows) for m in (0,) + near]
    score0, held = score([own] + by_near, blocks0, jnp.zeros((size, own_rows), jnp.float32))
    *by_far, score0, held = lax.optimization_barrier((*by_far, score0, held))
    band = jnp.concatenate(by_far, axis=0)
    foot = jnp.concatenate([own[cut:]] + [piece[cut:] for piece in by_near], axis=0)
    foot_far = [swap(foot, m) for m in far]
    band_near = [swap(band, m) for m in near]
    blocks1 = [(m, 0, cut) for m in far]
    score1, held = score([band], blocks1, held)
    barrier = lax.optimization_barrier((*foot_far, *band_near, score1, held))
    *pieces, score1, held = barrier
    blocks2 = [(f ^ m, cut, rest) for f in far for m in (0,) + near]
    blocks2 += [(f ^ m, 0, cut) for m in near for f in far]
    score2, value, _ = score(pieces, blocks2, held, last=True)
    scores = [score0, score1, score2]
    parts = [blocks0, blocks1, blocks2]
    held = [pltpu.VMEM((size, own_rows), jnp.float32)]
    flops = 8 * half_rows * pool_rows
    for step in range(ITERS):
        if step > 0:
            kernel = functools.partial(row_kernel, parts)
            (value,) = call(
                kernel, [(size, lines, LANES)], held, [me], [shift] + scores, flops, "rows"
            )
        value = lax.all_to_all(value, "pool", 0, 0, tiled=True)
        kernel = functools.partial(column_kernel, parts, log_a)
        value, potential = call(
            kernel,
            [(1, pool_rows), (size, own_rows)],
            [],
            [me],
            [value] + scores,
            flops,
            "columns",
        )
        pairs = [(i, i ^ 1) for i in range(2)]
        shift = log_b - log2_sum([value, lax.ppermute(value, "samp", pairs)])
    mine = lax.dynamic_slice_in_dim(potential, me[0], 1, 0)
    return mine * unit + own_norm[None, :], shift.reshape(pool_rows) * unit + pool_norm


def solution(mesh):
    placed = (
        P(("grp", "samp"), "pool", None),
        P(("grp", "pool"), None),
        P(("grp", "samp"), "pool", None, None),
        P(("grp", "samp"), "pool"),
    )
    return jax.shard_map(
        body,
        mesh=mesh,
        in_specs=placed,
        out_specs=(P(("grp", "samp"), "pool"), P(("grp", "pool"))),
        check_vma=False,
    )
```

```python
import functools
import math

import jax
import jax.numpy as jnp
from jax import lax
from jax.experimental import pallas as pl
from jax.experimental.pallas import tpu as pltpu
from jax.sharding import PartitionSpec as P

TILE = 512
CAP = 4
ITERS = 3


EPS = 0.02
NEG = -1e30
LN2 = math.log(2.0)
LANES = 128
SUBLANES = 8


def log2(value):
    return jnp.log(value) * (1.0 / LN2)


def log2_sum(values):
    peak = functools.reduce(jnp.maximum, values)
    total = functools.reduce(jnp.add, [jnp.exp2(v - peak) for v in values])
    return peak + log2(total)


def columns_of(width):
    return [slice(low, low + LANES) for low in range(0, width, LANES)]


def row_norms(ref):
    rows, width = ref.shape
    norms = []
    for low in range(0, rows, LANES):
        high = min(low + LANES, rows)
        folded = None
        for cut in columns_of(width):
            part = ref[low:high, cut].astype(jnp.float32)
            folded = part * part if folded is None else folded + part * part
        norms.append(jnp.sum(folded.T, axis=0, keepdims=True) * (1.0 / width))
    return norms[0] if len(norms) == 1 else jnp.concatenate(norms, axis=1)


def fill_scores(first, scale, owner_ref, list_ref, count_ref, piece_refs, pool_ref, joined, out):
    own_rows = piece_refs[0].shape[0]
    for k, ref in enumerate(piece_refs):
        joined[k * own_rows : (k + 1) * own_rows, :] = ref[...]
    dots = lax.dot_general(
        joined[...],
        pool_ref[...],
        (((1,), (1,)), ((), ())),
        preferred_element_type=jnp.float32,
    )
    for k in range(len(piece_refs)):
        tile = lax.div(owner_ref[first + k] * own_rows, TILE)
        rows = slice(k * own_rows, (k + 1) * own_rows)
        for u in range(pool_ref.shape[0] // TILE):
            counted = jnp.int32(0)
            for j in range(CAP):
                hit = (list_ref[0, 0, j, 0] == tile) & (list_ref[0, 0, j, 1] == u)
                counted += jnp.where(hit & (j < count_ref[0, 0]), 1, 0)
            offset = jnp.where(counted > 0, 0.0, NEG)
            cut = slice(u * TILE, (u + 1) * TILE)
            out[rows, cut] = dots[rows, cut] * scale + offset


def row_pass(first, owner_ref, shift, score_ref, held_ref):
    own_rows = held_ref.shape[1]
    across = LANES // own_rows
    for low in range(0, score_ref.shape[0], LANES):
        cuts = columns_of(score_ref.shape[1])
        rows = slice(low, low + LANES)
        peak = functools.reduce(jnp.maximum, [score_ref[rows, c] + shift[:, c] for c in cuts])
        terms = [jnp.exp2(score_ref[rows, c] + shift[:, c] - peak) for c in cuts]
        total = functools.reduce(jnp.add, terms)
        peak, total = peak.T, total.T
        top = jnp.max(peak, axis=0, keepdims=True)
        sums = top + log2(jnp.sum(total * jnp.exp2(peak - top), axis=0, keepdims=True))
        for k in range(across):
            owner = owner_ref[first + low // own_rows + k]
            held_ref[pl.ds(owner, 1), :] = sums[:, k * own_rows : (k + 1) * own_rows]


def copy_out(held_ref, out_ref):
    across = LANES // held_ref.shape[1]
    for line in range(out_ref.shape[1]):
        sources = [held_ref[line * across + k : line * across + k + 1, :] for k in range(across)]
        wide = jnp.concatenate(sources, axis=1)
        out_ref[:, line, :] = jnp.broadcast_to(wide, (out_ref.shape[0], LANES))


def early_kernel(count, scale, unit, owner_ref, list_ref, count_ref, *refs):
    pieces, pool_ref = refs[:count], refs[count]
    score_ref, held_ref, own_norm_ref, pool_norm_ref, joined = refs[count + 1 :]
    fill_scores(0, scale, owner_ref, list_ref, count_ref, pieces, pool_ref, joined, score_ref)
    own_norm_ref[...] = row_norms(pieces[0])
    norm = row_norms(pool_ref)
    pool_norm_ref[...] = norm
    held_ref[...] = jnp.zeros_like(held_ref)
    row_pass(0, owner_ref, norm * (-1.0 / unit), score_ref, held_ref)


def late_kernel(first, count, scale, unit, owner_ref, list_ref, count_ref, *refs):
    pieces, (pool_ref, norm_ref, before_ref) = refs[:count], refs[count : count + 3]
    score_ref, out_ref, joined, held_ref = refs[count + 3 :]
    fill_scores(first, scale, owner_ref, list_ref, count_ref, pieces, pool_ref, joined, score_ref)
    held_ref[...] = before_ref[...]
    row_pass(first, owner_ref, norm_ref[...] * (-1.0 / unit), score_ref, held_ref)
    copy_out(held_ref, out_ref)


def row_kernel(owner_ref, shift_ref, *refs):
    out_ref, held_ref = refs[-2:]
    shift = shift_ref[...]
    first = 0
    for ref in refs[:-2]:
        row_pass(first, owner_ref, shift, ref, held_ref)
        first += ref.shape[0] // held_ref.shape[1]
    copy_out(held_ref, out_ref)


def column_kernel(log_a, unit, owner_ref, value_ref, norm_ref, *refs):
    scores, (out_ref, own_ref, held_ref) = refs[:-3], refs[-3:]
    shift = log_a - log2_sum([value_ref[k] for k in range(value_ref.shape[0])])
    own_rows = held_ref.shape[1]
    across = LANES // own_rows
    for source in range(held_ref.shape[0]):
        line, place = source // across, source % across
        held_ref[source : source + 1, :] = shift[
            line : line + 1, place * own_rows : (place + 1) * own_rows
        ]
    own_ref[...] = held_ref[pl.ds(owner_ref[0], 1), :] * unit + norm_ref[...]
    cuts = columns_of(out_ref.shape[1])
    peaks = [jnp.full((SUBLANES, LANES), NEG, jnp.float32) for _ in cuts]
    spread = []
    k = 0
    for ref in scores:
        for low in range(0, ref.shape[0], LANES):
            rows = [held_ref[pl.ds(owner_ref[k + j], 1), :] for j in range(across)]
            k += across
            row = jnp.concatenate(rows, axis=1)
            spread.append(jnp.broadcast_to(row, (LANES, LANES)).T)
            for c, cut in enumerate(cuts):
                block = ref[low : low + LANES, cut] + spread[-1]
                block = block.reshape(LANES // SUBLANES, SUBLANES, LANES)
                peaks[c] = jnp.maximum(peaks[c], jnp.max(block, axis=0))
    totals = [jnp.zeros((SUBLANES, LANES), jnp.float32) for _ in cuts]
    for ref in scores:
        for low in range(0, ref.shape[0], LANES):
            add = spread.pop(0)
            for c, cut in enumerate(cuts):
                block = ref[low : low + LANES, cut] + add
                block = block.reshape(LANES // SUBLANES, SUBLANES, LANES)
                totals[c] += jnp.sum(jnp.exp2(block - peaks[c]), axis=0)
    for peak, total, cut in zip(peaks, totals, cuts):
        top = jnp.max(peak, axis=0, keepdims=True)
        out_ref[:, cut] = top + log2(jnp.sum(total * jnp.exp2(peak - top), axis=0, keepdims=True))


def call(kernel, shapes, scratch, scalars, arrays, flops, name):
    smem = pl.BlockSpec(memory_space=pltpu.SMEM)
    vmem = pl.BlockSpec(memory_space=pltpu.VMEM)
    moved = sum(a.size * a.dtype.itemsize for a in arrays) + 4 * sum(map(math.prod, shapes))
    return pl.pallas_call(
        kernel,
        out_shape=[jax.ShapeDtypeStruct(s, jnp.float32) for s in shapes],
        in_specs=[smem] * len(scalars) + [vmem] * len(arrays),
        out_specs=[vmem] * len(shapes),
        scratch_shapes=scratch,
        compiler_params=pltpu.CompilerParams(vmem_limit_bytes=3 * moved + (4 << 20)),
        cost_estimate=pl.CostEstimate(flops=flops, bytes_accessed=moved, transcendentals=0),
        name=name,
    )(*scalars, *arrays)


def body(samples, pool, tile_list, tile_count):
    own_rows, width = samples.shape[1:]
    size = lax.axis_size("pool")
    cores = lax.axis_size("samp")
    half_rows = own_rows * size
    pool_rows = pool.shape[0]
    lines = half_rows // LANES
    unit = EPS * LN2
    scale = 2.0 / (width * unit)
    log_a = -math.log2(half_rows * cores)
    log_b = -math.log2(pool_rows * size)
    own = samples.reshape(own_rows, width)

    def swap(value, masks):
        pairs = [
            (i * cores + c, (i ^ masks[c % 2]) * cores + c)
            for i in range(size)
            for c in range(cores)
        ]
        return lax.ppermute(value, ("pool", "samp"), pairs)

    def side_a(value):
        return swap(value, (1, 2))

    def side_b(value):
        return swap(value, (2, 1))

    def far(value, mask):
        return swap(value, (mask, mask))

    far12, far4 = far(own, 12), far(own, 4)
    a, b = side_a(own), side_b(own)
    corner = side_b(a)
    far8 = far(far12, 4)
    a4, b4 = side_a(far4), side_b(far4)
    a12, b12 = side_a(far12), side_b(far12)
    a8, b8 = side_a(far8), side_b(far8)
    corner12, corner4 = far(corner, 12), far(corner, 4)
    corner8 = far(corner12, 4)
    early = [own, a, b, corner, far4, far12, far8, a4, b4, a12, b12, b8]
    late = [a8, corner4, corner12, corner8]
    mask_a = 1 + lax.axis_index("samp") % 2
    mask_b = 3 - mask_a
    masks = [0, mask_a, mask_b, 3, 4, 12, 8, 4 + mask_a, 4 + mask_b, 12 + mask_a, 12 + mask_b]
    masks += [8 + mask_b, 8 + mask_a, 7, 15, 11]
    step = 16
    while step < size:
        late += [far(piece, step) for piece in early + late]
        masks += [m + step for m in masks]
        step *= 2
    owner = lax.axis_index("pool").astype(jnp.int32) ^ jnp.stack([jnp.int32(m) for m in masks])
    scalars = [owner, tile_list, tile_count]

    count = len(early)
    score0, held, own_norm, pool_norm = call(
        functools.partial(early_kernel, count, scale, unit),
        [(count * own_rows, pool_rows), (size, own_rows), (1, own_rows), (1, pool_rows)],
        [pltpu.VMEM((count * own_rows, width), samples.dtype)],
        scalars,
        early + [pool],
        2 * count * own_rows * pool_rows * width,
        "early_scores",
    )
    *late, score0, held, own_norm, pool_norm = lax.optimization_barrier(
        (*late, score0, held, own_norm, pool_norm)
    )
    rest = len(late)
    score1, value = call(
        functools.partial(late_kernel, count, rest, scale, unit),
        [(rest * own_rows, pool_rows), (size, lines, LANES)],
        [
            pltpu.VMEM((rest * own_rows, width), samples.dtype),
            pltpu.VMEM((size, own_rows), jnp.float32),
        ],
        scalars,
        late + [pool, pool_norm, held],
        2 * rest * own_rows * pool_rows * width,
        "late_scores",
    )
    scores = [score0, score1]
    flops = 8 * half_rows * pool_rows
    held = [pltpu.VMEM((size, own_rows), jnp.float32)]
    for iteration in range(ITERS):
        if iteration > 0:
            shapes = [(size, lines, LANES)]
            (value,) = call(row_kernel, shapes, held, [owner], [shift] + scores, flops, "rows")
        value = lax.all_to_all(value, "pool", 0, 0, tiled=True)
        value, sample_potential = call(
            functools.partial(column_kernel, log_a, unit),
            [(1, pool_rows), (1, own_rows)],
            held,
            [owner],
            [value, own_norm] + scores,
            flops,
            "columns",
        )
        pairs = [(i, i ^ 1) for i in range(cores)]
        shift = log_b - log2_sum([value, lax.ppermute(value, "samp", pairs)])
    return sample_potential, (shift * unit + pool_norm).reshape(pool_rows)


def solution(mesh):
    placed = (
        P(("grp", "samp"), "pool", None),
        P(("grp", "pool"), None),
        P(("grp", "samp"), "pool", None, None),
        P(("grp", "samp"), "pool"),
    )
    return jax.shard_map(
        body,
        mesh=mesh,
        in_specs=placed,
        out_specs=(P(("grp", "samp"), "pool"), P(("grp", "pool"))),
        check_vma=False,
    )
```

```python
import functools
import math

import jax
import jax.numpy as jnp
from jax import lax
from jax.experimental import pallas as pl
from jax.experimental.pallas import tpu as pltpu
from jax.sharding import PartitionSpec as P

TILE = 512
CAP = 4
ITERS = 3


EPS = 0.02
NEG = -1e30
LN2 = math.log(2.0)
LANES = 128
SUBLANES = 8


def log2(value):
    return jnp.log(value) * (1.0 / LN2)


def log2_sum(values):
    peak = functools.reduce(jnp.maximum, values)
    total = functools.reduce(jnp.add, [jnp.exp2(v - peak) for v in values])
    return peak + log2(total)


def columns_of(width):
    return [slice(low, low + LANES) for low in range(0, width, LANES)]


def row_norms(ref):
    rows, width = ref.shape
    norms = []
    for low in range(0, rows, LANES):
        high = min(low + LANES, rows)
        folded = None
        for cut in columns_of(width):
            part = ref[low:high, cut].astype(jnp.float32)
            folded = part * part if folded is None else folded + part * part
        norms.append(jnp.sum(folded.T, axis=0, keepdims=True) * (1.0 / width))
    return norms[0] if len(norms) == 1 else jnp.concatenate(norms, axis=1)


def fill_scores(first, size, scale, code_ref, piece_refs, pool_ref, joined, out):
    own_rows = piece_refs[0].shape[0]
    for k, ref in enumerate(piece_refs):
        joined[k * own_rows : (k + 1) * own_rows, :] = ref[...]
    dots = lax.dot_general(
        joined[...],
        pool_ref[...],
        (((1,), (1,)), ((), ())),
        preferred_element_type=jnp.float32,
    )
    for k in range(len(piece_refs)):
        rows = slice(k * own_rows, (k + 1) * own_rows)
        for u in range(pool_ref.shape[0] // TILE):
            offset = jnp.where((code_ref[first + k] & (size << u)) != 0, 0.0, NEG)
            cut = slice(u * TILE, (u + 1) * TILE)
            out[rows, cut] = dots[rows, cut] * scale + offset


def diagonal(size):
    rows = lax.broadcasted_iota(jnp.int32, (size, size), 0)
    return rows == lax.broadcasted_iota(jnp.int32, (size, size), 1)


def row_pass(first, code_ref, shift, score_ref, held_ref):
    size, own_rows = held_ref.shape
    eye = diagonal(own_rows)
    for k in range(score_ref.shape[0] // own_rows):
        block = score_ref[k * own_rows : (k + 1) * own_rows, :] + shift
        peak = jnp.max(block, axis=1, keepdims=True)
        total = jnp.sum(jnp.exp2(block - peak), axis=1, keepdims=True)
        sums = jnp.sum(jnp.where(eye, peak + log2(total), 0.0), axis=0, keepdims=True)
        held_ref[pl.ds(code_ref[first + k] & (size - 1), 1), :] = sums


def copy_out(held_ref, out_ref):
    across = LANES // held_ref.shape[1]
    for line in range(out_ref.shape[1]):
        sources = [held_ref[line * across + k : line * across + k + 1, :] for k in range(across)]
        wide = jnp.concatenate(sources, axis=1)
        out_ref[:, line, :] = jnp.broadcast_to(wide, (out_ref.shape[0], LANES))


def prepare_kernel(own_ref, pool_ref, own_out, pool_out, own_norm_ref, pool_norm_ref):
    own_out[...] = own_ref[...]
    pool_out[...] = pool_ref[...]
    own_norm_ref[...] = row_norms(own_ref)
    pool_norm_ref[...] = row_norms(pool_ref)


def early_kernel(count, scale, unit, code_ref, *refs):
    pieces, (pool_ref, norm_ref) = refs[:count], refs[count : count + 2]
    score_ref, held_ref, joined = refs[count + 2 :]
    size = held_ref.shape[0]
    fill_scores(0, size, scale, code_ref, pieces, pool_ref, joined, score_ref)
    held_ref[...] = jnp.zeros_like(held_ref)
    row_pass(0, code_ref, norm_ref[...] * (-1.0 / unit), score_ref, held_ref)


def late_kernel(first, count, scale, unit, code_ref, *refs):
    pieces, (pool_ref, norm_ref, before_ref) = refs[:count], refs[count : count + 3]
    score_ref, out_ref, joined, held_ref = refs[count + 3 :]
    size = held_ref.shape[0]
    fill_scores(first, size, scale, code_ref, pieces, pool_ref, joined, score_ref)
    held_ref[...] = before_ref[...]
    row_pass(first, code_ref, norm_ref[...] * (-1.0 / unit), score_ref, held_ref)
    copy_out(held_ref, out_ref)


def row_kernel(code_ref, shift_ref, *refs):
    out_ref, held_ref = refs[-2:]
    shift = shift_ref[...]
    first = 0
    for ref in refs[:-2]:
        row_pass(first, code_ref, shift, ref, held_ref)
        first += ref.shape[0] // held_ref.shape[1]
    copy_out(held_ref, out_ref)


def column_kernel(log_a, unit, code_ref, value_ref, norm_ref, *refs):
    scores, (out_ref, own_ref, held_ref) = refs[:-3], refs[-3:]
    shift = log_a - log2_sum([value_ref[k] for k in range(value_ref.shape[0])])
    size, own_rows = held_ref.shape
    pool_rows = out_ref.shape[1]
    across = LANES // own_rows
    for source in range(size):
        line, place = source // across, source % across
        held_ref[source : source + 1, :] = shift[
            line : line + 1, place * own_rows : (place + 1) * own_rows
        ]
    own_ref[...] = held_ref[pl.ds(code_ref[0] & (size - 1), 1), :] * unit + norm_ref[...]
    eye = diagonal(own_rows)
    folded = (own_rows // SUBLANES, SUBLANES, pool_rows)
    blocks = [
        (ref, slice(low, low + own_rows)) for ref in scores for low in range(0, ref.shape[0], own_rows)
    ]
    columns = []
    peak = None
    for k, (ref, rows) in enumerate(blocks):
        row = held_ref[pl.ds(code_ref[k] & (size - 1), 1), :]
        columns.append(jnp.sum(jnp.where(eye, row, 0.0), axis=1, keepdims=True))
        high = jnp.max((ref[rows, :] + columns[k]).reshape(folded), axis=0)
        peak = high if peak is None else jnp.maximum(peak, high)
    peak = jnp.max(peak, axis=0, keepdims=True)
    total = jnp.zeros((SUBLANES, pool_rows), jnp.float32)
    for k, (ref, rows) in enumerate(blocks):
        total += jnp.sum(jnp.exp2(ref[rows, :] + (columns[k] - peak)).reshape(folded), axis=0)
    out_ref[...] = peak + log2(jnp.sum(total, axis=0, keepdims=True))


def call(kernel, shapes, scratch, scalars, arrays, flops, name, dtypes=(jnp.float32,) * 4):
    smem = pl.BlockSpec(memory_space=pltpu.SMEM)
    vmem = pl.BlockSpec(memory_space=pltpu.VMEM)
    moved = sum(a.size * a.dtype.itemsize for a in arrays) + 4 * sum(map(math.prod, shapes))
    return pl.pallas_call(
        kernel,
        out_shape=[jax.ShapeDtypeStruct(s, d) for s, d in zip(shapes, dtypes)],
        in_specs=[smem] * len(scalars) + [vmem] * len(arrays),
        out_specs=[vmem] * len(shapes),
        scratch_shapes=scratch,
        compiler_params=pltpu.CompilerParams(vmem_limit_bytes=3 * moved + (4 << 20)),
        cost_estimate=pl.CostEstimate(flops=flops, bytes_accessed=moved, transcendentals=0),
        name=name,
    )(*scalars, *arrays)


def body(samples, pool, tile_list, tile_count):
    own_rows, width = samples.shape[1:]
    size = lax.axis_size("pool")
    cores = lax.axis_size("samp")
    half_rows = own_rows * size
    pool_rows = pool.shape[0]
    lines = half_rows // LANES
    unit = EPS * LN2
    scale = 2.0 / (width * unit)
    log_a = -math.log2(half_rows * cores)
    log_b = -math.log2(pool_rows * size)
    own = samples.reshape(own_rows, width)

    def swap(value, masks):
        pairs = [
            (i * cores + c, (i ^ masks[c % 2]) * cores + c)
            for i in range(size)
            for c in range(cores)
        ]
        return lax.ppermute(value, ("pool", "samp"), pairs)

    def side_a(value):
        return swap(value, (1, 2))

    def side_b(value):
        return swap(value, (2, 1))

    def far(value, mask):
        return swap(value, (mask, mask))

    own_copy, pool_copy, own_norm, pool_norm = call(
        prepare_kernel,
        [own.shape, pool.shape, (1, own_rows), (1, pool_rows)],
        [],
        [],
        [own, pool],
        4 * pool_rows * width,
        "prepare",
        (own.dtype, pool.dtype, jnp.float32, jnp.float32),
    )
    mask_a = 1 + lax.axis_index("samp").astype(jnp.int32) % 2
    mask_b = 3 - mask_a
    masks = [0, mask_a, mask_b, 3, 4, 12, 8, 4 + mask_a, 4 + mask_b, 12 + mask_a, 12 + mask_b]
    masks += [8 + mask_b, 8 + mask_a, 7, 15, 11]
    step = 16
    while step < size:
        masks += [m + step for m in masks]
        step *= 2
    owner = lax.axis_index("pool").astype(jnp.int32) ^ jnp.stack([jnp.int32(m) for m in masks])
    tile = owner * own_rows // TILE
    code = owner
    for u in range(pool_rows // TILE):
        for k in range(CAP):
            hit = (tile == tile_list[0, 0, k, 0]) & (tile_list[0, 0, k, 1] == u)
            code |= jnp.where(hit & (k < tile_count[0, 0]), size << u, 0)

    far12, far4 = far(own, 12), far(own, 4)
    a, b = side_a(own), side_b(own)
    corner = side_b(a)
    tied = lax.optimization_barrier((far12, code, own_copy, pool_copy, own_norm, pool_norm))
    far12, code, own_copy, pool_copy, own_norm, pool_norm = tied
    far8 = far(far12, 4)
    a4, b4 = side_a(far4), side_b(far4)
    a12, b12 = side_a(far12), side_b(far12)
    a8, b8 = side_a(far8), side_b(far8)
    corner12, corner4 = far(corner, 12), far(corner, 4)
    corner8 = far(corner12, 4)
    early = [own_copy, a, b, corner, far4, far12, far8, a4, b4, a12, b12, b8]
    late = [a8, corner4, corner12, corner8]
    step = 16
    while step < size:
        late += [far(piece, step) for piece in early + late]
        step *= 2
    count = len(early)
    score0, held = call(
        functools.partial(early_kernel, count, scale, unit),
        [(count * own_rows, pool_rows), (size, own_rows)],
        [pltpu.VMEM((count * own_rows, width), samples.dtype)],
        [code],
        early + [pool_copy, pool_norm],
        2 * count * own_rows * pool_rows * width,
        "early_scores",
    )
    *late, score0, held = lax.optimization_barrier((*late, score0, held))
    rest = len(late)
    score1, value = call(
        functools.partial(late_kernel, count, rest, scale, unit),
        [(rest * own_rows, pool_rows), (size, lines, LANES)],
        [
            pltpu.VMEM((rest * own_rows, width), samples.dtype),
            pltpu.VMEM((size, own_rows), jnp.float32),
        ],
        [code],
        late + [pool_copy, pool_norm, held],
        2 * rest * own_rows * pool_rows * width,
        "late_scores",
    )
    scores = [score0, score1]
    flops = 8 * half_rows * pool_rows
    held = [pltpu.VMEM((size, own_rows), jnp.float32)]
    for iteration in range(ITERS):
        if iteration > 0:
            shapes = [(size, lines, LANES)]
            (value,) = call(row_kernel, shapes, held, [code], [shift] + scores, flops, "rows")
        value = lax.all_to_all(value, "pool", 0, 0, tiled=True)
        value, sample_potential = call(
            functools.partial(column_kernel, log_a, unit),
            [(1, pool_rows), (1, own_rows)],
            held,
            [code],
            [value, own_norm] + scores,
            flops,
            "columns",
        )
        pairs = [(i, i ^ 1) for i in range(cores)]
        shift = log_b - log2_sum([value, lax.ppermute(value, "samp", pairs)])
    return sample_potential, (shift * unit + pool_norm).reshape(pool_rows)


def solution(mesh):
    placed = (
        P(("grp", "samp"), "pool", None),
        P(("grp", "pool"), None),
        P(("grp", "samp"), "pool", None, None),
        P(("grp", "samp"), "pool"),
    )
    return jax.shard_map(
        body,
        mesh=mesh,
        in_specs=placed,
        out_specs=(P(("grp", "samp"), "pool"), P(("grp", "pool"))),
        check_vma=False,
    )
```

```python
import functools
import math

import jax
import jax.numpy as jnp
from jax import lax
from jax.experimental import pallas as pl
from jax.experimental.pallas import tpu as pltpu
from jax.sharding import PartitionSpec as P

TILE = 512
CAP = 4
ITERS = 3


EPS = 0.02
NEG = -1e30
LN2 = math.log(2.0)
LANES = 128
SUBLANES = 8


def log2(value):
    return jnp.log(value) * (1.0 / LN2)


def log2_sum(values):
    peak = functools.reduce(jnp.maximum, values)
    total = functools.reduce(jnp.add, [jnp.exp2(v - peak) for v in values])
    return peak + log2(total)


def owner_of(id_ref, piece):
    near, far = piece
    side = id_ref[0] & 1
    mask = (0, 1 + side, 2 - side, 3)[near] + far
    return lax.shift_right_logical(id_ref[0], 1) ^ mask


def columns_of(width):
    return [slice(low, low + LANES) for low in range(0, width, LANES)]


def row_norms(block):
    rows, width = block.shape
    folded = None
    for cut in columns_of(width):
        part = block[:, cut].astype(jnp.float32)
        folded = part * part if folded is None else folded + part * part
    return jnp.sum(folded.T, axis=0, keepdims=True) * (1.0 / width)


def fill_scores(pieces, scale, id_ref, piece_refs, pool_ref, mask_ref, joined, out):
    own_rows = piece_refs[0].shape[0]
    for k, ref in enumerate(piece_refs):
        joined[k * own_rows : (k + 1) * own_rows, :] = ref[...]
    dots = lax.dot_general(
        joined[...],
        pool_ref[...],
        (((1,), (1,)), ((), ())),
        preferred_element_type=jnp.float32,
    )
    for k, piece in enumerate(pieces):
        rows = slice(k * own_rows, (k + 1) * own_rows)
        tile = lax.div(owner_of(id_ref, piece) * own_rows, TILE)
        out[rows, :] = dots[rows, :] * scale + mask_ref[pl.ds(tile, 1), :]


def diagonal(size):
    rows = lax.broadcasted_iota(jnp.int32, (size, size), 0)
    return rows == lax.broadcasted_iota(jnp.int32, (size, size), 1)


def row_pass(pieces, id_ref, shift, score_ref, held_ref):
    own_rows = held_ref.shape[1]
    eye = diagonal(own_rows)
    for k, piece in enumerate(pieces):
        block = score_ref[k * own_rows : (k + 1) * own_rows, :] + shift
        peak = jnp.max(block, axis=1, keepdims=True)
        total = jnp.sum(jnp.exp2(block - peak), axis=1, keepdims=True)
        sums = jnp.sum(jnp.where(eye, peak + log2(total), 0.0), axis=0, keepdims=True)
        held_ref[pl.ds(owner_of(id_ref, piece), 1), :] = sums


def copy_out(held_ref, out_ref):
    across = LANES // held_ref.shape[1]
    for line in range(out_ref.shape[1]):
        sources = [held_ref[line * across + k : line * across + k + 1, :] for k in range(across)]
        wide = jnp.concatenate(sources, axis=1)
        out_ref[:, line, :] = jnp.broadcast_to(wide, (out_ref.shape[0], LANES))


def prepare_kernel(list_ref, count_ref, own_ref, pool_ref, *refs):
    own_out, pool_out, own_norm_ref, pool_norm_ref, mask_ref, own_sem, pool_sem = refs
    own_copy = pltpu.make_async_copy(own_ref, own_out, own_sem)
    own_copy.start()
    pool_rows = pool_ref.shape[0]
    step = pool_rows // pool_sem.shape[0]
    copies = []
    for k in range(pool_sem.shape[0]):
        rows = pl.ds(k * step, step)
        copies.append(
            pltpu.make_async_copy(pool_ref.at[rows], pool_out.at[rows], pool_sem.at[k])
        )
        copies[-1].start()
    for t in range(mask_ref.shape[0]):
        for u in range(pool_rows // TILE):
            counted = jnp.int32(0)
            for k in range(CAP):
                hit = (list_ref[0, 0, k, 0] == t) & (list_ref[0, 0, k, 1] == u)
                counted += jnp.where(hit & (k < count_ref[0, 0]), 1, 0)
            offset = jnp.where(counted > 0, 0.0, NEG)
            mask_ref[t : t + 1, u * TILE : (u + 1) * TILE] = jnp.full((1, TILE), offset)
    own_copy.wait()
    own_norm_ref[...] = row_norms(own_out[...])
    for k, copy in enumerate(copies):
        copy.wait()
        for low in range(k * step, (k + 1) * step, LANES):
            rows = slice(low, low + LANES)
            pool_norm_ref[:, rows] = row_norms(pool_out[rows, :])


def early_kernel(pieces, scale, unit, id_ref, *refs):
    count = len(pieces)
    piece_refs, (pool_ref, norm_ref, mask_ref) = refs[:count], refs[count : count + 3]
    score_ref, held_ref, joined = refs[count + 3 :]
    fill_scores(pieces, scale, id_ref, piece_refs, pool_ref, mask_ref, joined, score_ref)
    held_ref[...] = jnp.zeros_like(held_ref)
    row_pass(pieces, id_ref, norm_ref[...] * (-1.0 / unit), score_ref, held_ref)


def late_kernel(pieces, scale, unit, id_ref, *refs):
    count = len(pieces)
    piece_refs, (pool_ref, norm_ref, mask_ref) = refs[:count], refs[count : count + 3]
    before_ref, score_ref, out_ref, joined, held_ref = refs[count + 3 :]
    fill_scores(pieces, scale, id_ref, piece_refs, pool_ref, mask_ref, joined, score_ref)
    held_ref[...] = before_ref[...]
    row_pass(pieces, id_ref, norm_ref[...] * (-1.0 / unit), score_ref, held_ref)
    copy_out(held_ref, out_ref)


def row_kernel(parts, id_ref, shift_ref, *refs):
    out_ref, held_ref = refs[-2:]
    shift = shift_ref[...]
    for ref, pieces in zip(refs[:-2], parts):
        row_pass(pieces, id_ref, shift, ref, held_ref)
    copy_out(held_ref, out_ref)


def column_kernel(parts, log_a, unit, id_ref, value_ref, norm_ref, *refs):
    scores, (out_ref, own_ref, held_ref) = refs[:-3], refs[-3:]
    shift = log_a - log2_sum([value_ref[k] for k in range(value_ref.shape[0])])
    size, own_rows = held_ref.shape
    pool_rows = out_ref.shape[1]
    across = LANES // own_rows
    for source in range(size):
        line, place = source // across, source % across
        held_ref[source : source + 1, :] = shift[
            line : line + 1, place * own_rows : (place + 1) * own_rows
        ]
    own_ref[...] = held_ref[pl.ds(owner_of(id_ref, (0, 0)), 1), :] * unit + norm_ref[...]
    eye = diagonal(own_rows)
    folded = (own_rows // SUBLANES, SUBLANES, pool_rows)
    blocks = [
        (ref, slice(k * own_rows, (k + 1) * own_rows), piece)
        for ref, pieces in zip(scores, parts)
        for k, piece in enumerate(pieces)
    ]
    columns = []
    peak = None
    for k, (ref, rows, piece) in enumerate(blocks):
        row = held_ref[pl.ds(owner_of(id_ref, piece), 1), :]
        columns.append(jnp.sum(jnp.where(eye, row, 0.0), axis=1, keepdims=True))
        high = jnp.max((ref[rows, :] + columns[k]).reshape(folded), axis=0)
        peak = high if peak is None else jnp.maximum(peak, high)
    peak = jnp.max(peak, axis=0, keepdims=True)
    total = jnp.zeros((SUBLANES, pool_rows), jnp.float32)
    for k, (ref, rows, _) in enumerate(blocks):
        total += jnp.sum(jnp.exp2(ref[rows, :] + (columns[k] - peak)).reshape(folded), axis=0)
    out_ref[...] = peak + log2(jnp.sum(total, axis=0, keepdims=True))


def call(kernel, shapes, scratch, scalars, arrays, flops, name):
    smem = pl.BlockSpec(memory_space=pltpu.SMEM)
    vmem = pl.BlockSpec(memory_space=pltpu.VMEM)
    moved = sum(a.size * a.dtype.itemsize for a in arrays) + 4 * sum(map(math.prod, shapes))
    return pl.pallas_call(
        kernel,
        out_shape=[jax.ShapeDtypeStruct(s, jnp.float32) for s in shapes],
        in_specs=[smem] * len(scalars) + [vmem] * len(arrays),
        out_specs=[vmem] * len(shapes),
        scratch_shapes=scratch,
        compiler_params=pltpu.CompilerParams(vmem_limit_bytes=3 * moved + (4 << 20)),
        cost_estimate=pl.CostEstimate(flops=flops, bytes_accessed=moved, transcendentals=0),
        name=name,
    )(*scalars, *arrays)


def prepare(tile_list, tile_count, own, pool, tiles):
    smem = pl.BlockSpec(memory_space=pltpu.SMEM)
    vmem = pl.BlockSpec(memory_space=pltpu.VMEM)
    chunks = 4
    shapes = [
        jax.ShapeDtypeStruct(own.shape, own.dtype),
        jax.ShapeDtypeStruct(pool.shape, pool.dtype),
        jax.ShapeDtypeStruct((1, own.shape[0]), jnp.float32),
        jax.ShapeDtypeStruct((1, pool.shape[0]), jnp.float32),
        jax.ShapeDtypeStruct((tiles, pool.shape[0]), jnp.float32),
    ]
    return pl.pallas_call(
        prepare_kernel,
        out_shape=shapes,
        in_specs=[smem, smem] + [pl.BlockSpec(memory_space=pl.ANY)] * 2,
        out_specs=[vmem] * len(shapes),
        scratch_shapes=[pltpu.SemaphoreType.DMA, pltpu.SemaphoreType.DMA((chunks,))],
        compiler_params=pltpu.CompilerParams(vmem_limit_bytes=16 << 20),
        cost_estimate=pl.CostEstimate(
            flops=2 * pool.size, bytes_accessed=4 * pool.size, transcendentals=0
        ),
        name="prepare",
    )(tile_list, tile_count, own, pool)


def body(samples, pool, tile_list, tile_count):
    own_rows, width = samples.shape[1:]
    size = lax.axis_size("pool")
    cores = lax.axis_size("samp")
    half_rows = own_rows * size
    pool_rows = pool.shape[0]
    lines = half_rows // LANES
    unit = EPS * LN2
    scale = 2.0 / (width * unit)
    log_a = -math.log2(half_rows * cores)
    log_b = -math.log2(pool_rows * size)
    own = samples.reshape(own_rows, width)

    def swap(value, masks):
        pairs = [
            (i * cores + c, (i ^ masks[c % 2]) * cores + c)
            for i in range(size)
            for c in range(cores)
        ]
        return lax.ppermute(value, ("pool", "samp"), pairs)

    def side_a(value):
        return swap(value, (1, 2))

    def side_b(value):
        return swap(value, (2, 1))

    def far(value, mask):
        return swap(value, (mask, mask))

    local = prepare(tile_list, tile_count, own, pool, half_rows // TILE)
    index = lax.axis_index("pool") * 2 + lax.axis_index("samp") % 2
    ids = [index.astype(jnp.int32).reshape(1)]

    far12, far4 = far(own, 12), far(own, 4)
    a, b = side_a(own), side_b(own)
    corner = side_b(a)
    far12, *local = lax.optimization_barrier((far12, *local))
    own_copy, pool_copy, own_norm, pool_norm, mask = local
    far8 = far(far12, 4)
    a4, b4 = side_a(far4), side_b(far4)
    a12, b12 = side_a(far12), side_b(far12)
    a8, b8 = side_a(far8), side_b(far8)
    corner12, corner4 = far(corner, 12), far(corner, 4)
    corner8 = far(corner12, 4)
    early = [own_copy, a, b, corner, far4, far12, far8, a4, b4, a12, b12, b8]
    early_pieces = [(0, 0), (1, 0), (2, 0), (3, 0), (0, 4), (0, 12), (0, 8)]
    early_pieces += [(1, 4), (2, 4), (1, 12), (2, 12), (2, 8)]
    late = [a8, corner4, corner12, corner8]
    late_pieces = [(1, 8), (3, 4), (3, 12), (3, 8)]
    step = 16
    while step < size:
        late += [far(piece, step) for piece in early + late]
        late_pieces += [(near, z + step) for near, z in early_pieces + late_pieces]
        step *= 2

    count = len(early) * own_rows
    score0, held = call(
        functools.partial(early_kernel, early_pieces, scale, unit),
        [(count, pool_rows), (size, own_rows)],
        [pltpu.VMEM((count, width), samples.dtype)],
        ids,
        early + [pool_copy, pool_norm, mask],
        2 * count * pool_rows * width,
        "early_scores",
    )
    *late, score0, held = lax.optimization_barrier((*late, score0, held))
    count = len(late) * own_rows
    score1, value = call(
        functools.partial(late_kernel, late_pieces, scale, unit),
        [(count, pool_rows), (size, lines, LANES)],
        [
            pltpu.VMEM((count, width), samples.dtype),
            pltpu.VMEM((size, own_rows), jnp.float32),
        ],
        ids,
        late + [pool_copy, pool_norm, mask, held],
        2 * count * pool_rows * width,
        "late_scores",
    )
    parts = [early_pieces, late_pieces]
    scores = [score0, score1]
    flops = 8 * half_rows * pool_rows
    held = [pltpu.VMEM((size, own_rows), jnp.float32)]
    for iteration in range(ITERS):
        if iteration > 0:
            kernel = functools.partial(row_kernel, parts)
            shapes = [(size, lines, LANES)]
            (value,) = call(kernel, shapes, held, ids, [shift] + scores, flops, "rows")
        value = lax.all_to_all(value, "pool", 0, 0, tiled=True)
        value, sample_potential = call(
            functools.partial(column_kernel, parts, log_a, unit),
            [(1, pool_rows), (1, own_rows)],
            held,
            ids,
            [value, own_norm] + scores,
            flops,
            "columns",
        )
        pairs = [(i, i ^ 1) for i in range(cores)]
        shift = log_b - log2_sum([value, lax.ppermute(value, "samp", pairs)])
    return sample_potential, (shift * unit + pool_norm).reshape(pool_rows)


def solution(mesh):
    placed = (
        P(("grp", "samp"), "pool", None),
        P(("grp", "pool"), None),
        P(("grp", "samp"), "pool", None, None),
        P(("grp", "samp"), "pool"),
    )
    return jax.shard_map(
        body,
        mesh=mesh,
        in_specs=placed,
        out_specs=(P(("grp", "samp"), "pool"), P(("grp", "pool"))),
        check_vma=False,
    )
```

```python
import functools
import math

import jax
import jax.numpy as jnp
from jax import lax
from jax.experimental import pallas as pl
from jax.experimental.pallas import tpu as pltpu
from jax.sharding import PartitionSpec as P

TILE = 512
CAP = 4
ITERS = 3


EPS = 0.02
NEG = -1e30
LN2 = math.log(2.0)
LANES = 128
SUBLANES = 8


def log2(value):
    return jnp.log(value) * (1.0 / LN2)


def log2_sum(values):
    peak = functools.reduce(jnp.maximum, values)
    total = functools.reduce(jnp.add, [jnp.exp2(v - peak) for v in values])
    return peak + log2(total)


def owner_of(id_ref, piece):
    near, far = piece
    side = id_ref[0] & 1
    mask = (0, 1 + side, 2 - side, 3)[near] + far
    return lax.shift_right_logical(id_ref[0], 1) ^ mask


def columns_of(width):
    return [slice(low, low + LANES) for low in range(0, width, LANES)]


def row_norms(block):
    rows, width = block.shape
    folded = None
    for cut in columns_of(width):
        part = block[:, cut].astype(jnp.float32)
        folded = part * part if folded is None else folded + part * part
    return jnp.sum(folded.T, axis=0, keepdims=True) * (1.0 / width)


def fill_scores(pieces, scale, id_ref, piece_refs, pool_ref, mask_ref, joined, out):
    own_rows = piece_refs[0].shape[0]
    for k, ref in enumerate(piece_refs):
        joined[k * own_rows : (k + 1) * own_rows, :] = ref[...]
    dots = lax.dot_general(
        joined[...],
        pool_ref[...],
        (((1,), (1,)), ((), ())),
        preferred_element_type=jnp.float32,
    )
    for k, piece in enumerate(pieces):
        rows = slice(k * own_rows, (k + 1) * own_rows)
        tile = lax.div(owner_of(id_ref, piece) * own_rows, TILE)
        out[rows, :] = dots[rows, :] * scale + mask_ref[pl.ds(tile, 1), :]


def diagonal(size):
    rows = lax.broadcasted_iota(jnp.int32, (size, size), 0)
    return rows == lax.broadcasted_iota(jnp.int32, (size, size), 1)


def row_pass(pieces, id_ref, shift, score_ref, held_ref):
    own_rows = held_ref.shape[1]
    eye = diagonal(own_rows)
    for k, piece in enumerate(pieces):
        block = score_ref[k * own_rows : (k + 1) * own_rows, :] + shift
        peak = jnp.max(block, axis=1, keepdims=True)
        total = jnp.sum(jnp.exp2(block - peak), axis=1, keepdims=True)
        sums = jnp.sum(jnp.where(eye, peak + log2(total), 0.0), axis=0, keepdims=True)
        held_ref[pl.ds(owner_of(id_ref, piece), 1), :] = sums


def copy_out(held_ref, out_ref):
    across = LANES // held_ref.shape[1]
    for line in range(out_ref.shape[1]):
        sources = [held_ref[line * across + k : line * across + k + 1, :] for k in range(across)]
        wide = jnp.concatenate(sources, axis=1)
        out_ref[:, line, :] = jnp.broadcast_to(wide, (out_ref.shape[0], LANES))


def prepare_kernel(list_hbm, count_hbm, own_ref, pool_ref, *refs):
    own_out, pool_out, own_norm_ref, pool_norm_ref, mask_ref = refs[:5]
    list_ref, count_ref, list_sem, count_sem, own_sem, pool_sem = refs[5:]
    list_copy = pltpu.make_async_copy(list_hbm, list_ref, list_sem)
    count_copy = pltpu.make_async_copy(count_hbm, count_ref, count_sem)
    list_copy.start()
    count_copy.start()
    own_copy = pltpu.make_async_copy(own_ref, own_out, own_sem)
    own_copy.start()
    pool_rows = pool_ref.shape[0]
    step = pool_rows // pool_sem.shape[0]
    copies = []
    for k in range(pool_sem.shape[0]):
        rows = pl.ds(k * step, step)
        copies.append(
            pltpu.make_async_copy(pool_ref.at[rows], pool_out.at[rows], pool_sem.at[k])
        )
        copies[-1].start()
    list_copy.wait()
    count_copy.wait()
    for t in range(mask_ref.shape[0]):
        for u in range(pool_rows // TILE):
            counted = jnp.int32(0)
            for k in range(CAP):
                hit = (list_ref[0, 0, 0, k] == t) & (list_ref[0, 0, 1, k] == u)
                counted += jnp.where(hit & (k < count_ref[0, 0]), 1, 0)
            offset = jnp.where(counted > 0, 0.0, NEG)
            mask_ref[t : t + 1, u * TILE : (u + 1) * TILE] = jnp.full((1, TILE), offset)
    own_copy.wait()
    own_norm_ref[...] = row_norms(own_out[...])
    for k, copy in enumerate(copies):
        copy.wait()
        for low in range(k * step, (k + 1) * step, LANES):
            rows = slice(low, low + LANES)
            pool_norm_ref[:, rows] = row_norms(pool_out[rows, :])


def early_kernel(pieces, scale, unit, id_ref, *refs):
    count = len(pieces)
    piece_refs, (pool_ref, norm_ref, mask_ref) = refs[:count], refs[count : count + 3]
    score_ref, held_ref, joined = refs[count + 3 :]
    fill_scores(pieces, scale, id_ref, piece_refs, pool_ref, mask_ref, joined, score_ref)
    held_ref[...] = jnp.zeros_like(held_ref)
    row_pass(pieces, id_ref, norm_ref[...] * (-1.0 / unit), score_ref, held_ref)


def late_kernel(pieces, scale, unit, id_ref, *refs):
    count = len(pieces)
    piece_refs, (pool_ref, norm_ref, mask_ref) = refs[:count], refs[count : count + 3]
    before_ref, score_ref, out_ref, joined, held_ref = refs[count + 3 :]
    fill_scores(pieces, scale, id_ref, piece_refs, pool_ref, mask_ref, joined, score_ref)
    held_ref[...] = before_ref[...]
    row_pass(pieces, id_ref, norm_ref[...] * (-1.0 / unit), score_ref, held_ref)
    copy_out(held_ref, out_ref)


def row_kernel(parts, id_ref, shift_ref, *refs):
    out_ref, held_ref = refs[-2:]
    shift = shift_ref[...]
    for ref, pieces in zip(refs[:-2], parts):
        row_pass(pieces, id_ref, shift, ref, held_ref)
    copy_out(held_ref, out_ref)


def column_kernel(parts, log_a, unit, id_ref, value_ref, norm_ref, *refs):
    scores, (out_ref, own_ref, held_ref) = refs[:-3], refs[-3:]
    shift = log_a - log2_sum([value_ref[k] for k in range(value_ref.shape[0])])
    size, own_rows = held_ref.shape
    pool_rows = out_ref.shape[1]
    across = LANES // own_rows
    for source in range(size):
        line, place = source // across, source % across
        held_ref[source : source + 1, :] = shift[
            line : line + 1, place * own_rows : (place + 1) * own_rows
        ]
    own = held_ref[pl.ds(owner_of(id_ref, (0, 0)), 1), :] * unit + norm_ref[...]
    own_ref[...] = jnp.broadcast_to(jnp.concatenate([own] * across, axis=1), own_ref.shape)
    eye = diagonal(own_rows)
    folded = (own_rows // SUBLANES, SUBLANES, pool_rows)
    blocks = [
        (ref, slice(k * own_rows, (k + 1) * own_rows), piece)
        for ref, pieces in zip(scores, parts)
        for k, piece in enumerate(pieces)
    ]
    columns = []
    peak = None
    for k, (ref, rows, piece) in enumerate(blocks):
        row = held_ref[pl.ds(owner_of(id_ref, piece), 1), :]
        columns.append(jnp.sum(jnp.where(eye, row, 0.0), axis=1, keepdims=True))
        high = jnp.max((ref[rows, :] + columns[k]).reshape(folded), axis=0)
        peak = high if peak is None else jnp.maximum(peak, high)
    peak = jnp.max(peak, axis=0, keepdims=True)
    total = jnp.zeros((SUBLANES, pool_rows), jnp.float32)
    for k, (ref, rows, _) in enumerate(blocks):
        total += jnp.sum(jnp.exp2(ref[rows, :] + (columns[k] - peak)).reshape(folded), axis=0)
    out_ref[...] = peak + log2(jnp.sum(total, axis=0, keepdims=True))


def call(kernel, shapes, scratch, scalars, arrays, flops, name):
    smem = pl.BlockSpec(memory_space=pltpu.SMEM)
    vmem = pl.BlockSpec(memory_space=pltpu.VMEM)
    moved = sum(a.size * a.dtype.itemsize for a in arrays) + 4 * sum(map(math.prod, shapes))
    return pl.pallas_call(
        kernel,
        out_shape=[jax.ShapeDtypeStruct(s, jnp.float32) for s in shapes],
        in_specs=[smem] * len(scalars) + [vmem] * len(arrays),
        out_specs=[vmem] * len(shapes),
        scratch_shapes=scratch,
        compiler_params=pltpu.CompilerParams(vmem_limit_bytes=3 * moved + (4 << 20)),
        cost_estimate=pl.CostEstimate(flops=flops, bytes_accessed=moved, transcendentals=0),
        name=name,
    )(*scalars, *arrays)


def prepare(tile_list, tile_count, own, pool, tiles):
    vmem = pl.BlockSpec(memory_space=pltpu.VMEM)
    chunks = 4
    shapes = [
        jax.ShapeDtypeStruct(own.shape, own.dtype),
        jax.ShapeDtypeStruct(pool.shape, pool.dtype),
        jax.ShapeDtypeStruct((1, own.shape[0]), jnp.float32),
        jax.ShapeDtypeStruct((1, pool.shape[0]), jnp.float32),
        jax.ShapeDtypeStruct((tiles, pool.shape[0]), jnp.float32),
    ]
    return pl.pallas_call(
        prepare_kernel,
        out_shape=shapes,
        in_specs=[pl.BlockSpec(memory_space=pltpu.HBM)] * 4,
        out_specs=[vmem] * len(shapes),
        scratch_shapes=[
            pltpu.SMEM(tile_list.shape, jnp.int32),
            pltpu.SMEM(tile_count.shape, jnp.int32),
            pltpu.SemaphoreType.DMA,
            pltpu.SemaphoreType.DMA,
            pltpu.SemaphoreType.DMA,
            pltpu.SemaphoreType.DMA((chunks,)),
        ],
        compiler_params=pltpu.CompilerParams(vmem_limit_bytes=16 << 20),
        cost_estimate=pl.CostEstimate(
            flops=2 * pool.size, bytes_accessed=4 * pool.size, transcendentals=0
        ),
        name="prepare",
    )(tile_list, tile_count, own, pool)


def body(samples, pool, tile_list, tile_count):
    own_rows, width = samples.shape[1:]
    size = lax.axis_size("pool")
    cores = lax.axis_size("samp")
    half_rows = own_rows * size
    pool_rows = pool.shape[0]
    lines = half_rows // LANES
    unit = EPS * LN2
    scale = 2.0 / (width * unit)
    log_a = -math.log2(half_rows * cores)
    log_b = -math.log2(pool_rows * size)
    own = samples.reshape(own_rows, width)

    def swap(value, masks):
        pairs = [
            (i * cores + c, (i ^ masks[c % 2]) * cores + c)
            for i in range(size)
            for c in range(cores)
        ]
        return lax.ppermute(value, ("pool", "samp"), pairs)

    def side_a(value):
        return swap(value, (1, 2))

    def side_b(value):
        return swap(value, (2, 1))

    def far(value, mask):
        return swap(value, (mask, mask))

    index = lax.axis_index("pool") * 2 + lax.axis_index("samp") % 2
    ids = [index.astype(jnp.int32).reshape(1)]

    far12, far4 = far(own, 12), far(own, 4)
    a, b = side_a(own), side_b(own)
    corner = swap(own, (3, 3))
    pairs = tile_list.swapaxes(2, 3)
    local = prepare(pairs, tile_count, own, pool, half_rows // TILE)
    far12, *local = lax.optimization_barrier((far12, *local))
    own_copy, pool_copy, own_norm, pool_norm, mask = local
    far8 = far(far12, 4)
    a4, b4 = side_a(far4), side_b(far4)
    a12, b12 = side_a(far12), side_b(far12)
    a8, b8 = side_a(far8), side_b(far8)
    corner12, corner4 = far(corner, 12), far(corner, 4)
    corner8 = far(corner12, 4)
    early = [own_copy, a, b, corner, far4, far12, far8, a4, b4, a12, b12, b8]
    early_pieces = [(0, 0), (1, 0), (2, 0), (3, 0), (0, 4), (0, 12), (0, 8)]
    early_pieces += [(1, 4), (2, 4), (1, 12), (2, 12), (2, 8)]
    late = [a8, corner4, corner12, corner8]
    late_pieces = [(1, 8), (3, 4), (3, 12), (3, 8)]
    step = 16
    while step < size:
        late += [far(piece, step) for piece in early + late]
        late_pieces += [(near, z + step) for near, z in early_pieces + late_pieces]
        step *= 2

    count = len(early) * own_rows
    score0, held = call(
        functools.partial(early_kernel, early_pieces, scale, unit),
        [(count, pool_rows), (size, own_rows)],
        [pltpu.VMEM((count, width), samples.dtype)],
        ids,
        early + [pool_copy, pool_norm, mask],
        2 * count * pool_rows * width,
        "early_scores",
    )
    *late, score0, held = lax.optimization_barrier((*late, score0, held))
    count = len(late) * own_rows
    score1, value = call(
        functools.partial(late_kernel, late_pieces, scale, unit),
        [(count, pool_rows), (size, lines, LANES)],
        [
            pltpu.VMEM((count, width), samples.dtype),
            pltpu.VMEM((size, own_rows), jnp.float32),
        ],
        ids,
        late + [pool_copy, pool_norm, mask, held],
        2 * count * pool_rows * width,
        "late_scores",
    )
    parts = [early_pieces, late_pieces]
    scores = [score0, score1]
    flops = 8 * half_rows * pool_rows
    held = [pltpu.VMEM((size, own_rows), jnp.float32)]
    for iteration in range(ITERS):
        if iteration > 0:
            kernel = functools.partial(row_kernel, parts)
            shapes = [(size, lines, LANES)]
            (value,) = call(kernel, shapes, held, ids, [shift] + scores, flops, "rows")
        value = lax.all_to_all(value, "pool", 0, 0, tiled=True)
        value, sample_potential = call(
            functools.partial(column_kernel, parts, log_a, unit),
            [(1, pool_rows), (SUBLANES, LANES)],
            held,
            ids,
            [value, own_norm] + scores,
            flops,
            "columns",
        )
        pairs = [(i, i ^ 1) for i in range(cores)]
        shift = log_b - log2_sum([value, lax.ppermute(value, "samp", pairs)])
    return sample_potential[:1, :own_rows], (shift * unit + pool_norm).reshape(pool_rows)


def solution(mesh):
    placed = (
        P(("grp", "samp"), "pool", None),
        P(("grp", "pool"), None),
        P(("grp", "samp"), "pool", None, None),
        P(("grp", "samp"), "pool"),
    )
    return jax.shard_map(
        body,
        mesh=mesh,
        in_specs=placed,
        out_specs=(P(("grp", "samp"), "pool"), P(("grp", "pool"))),
        check_vma=False,
    )
```

```python
import functools
import math

import jax
import jax.numpy as jnp
from jax import lax
from jax.experimental import pallas as pl
from jax.experimental.pallas import tpu as pltpu
from jax.sharding import PartitionSpec as P

TILE = 512
CAP = 4
ITERS = 3


EPS = 0.02
NEG = -1e30
LN2 = math.log(2.0)
LANES = 128
SUBLANES = 8


def log2(value):
    return jnp.log(value) * (1.0 / LN2)


def log2_sum(values):
    peak = functools.reduce(jnp.maximum, values)
    total = functools.reduce(jnp.add, [jnp.exp2(v - peak) for v in values])
    return peak + log2(total)


def owner_of(id_ref, piece):
    near, far = piece
    side = id_ref[0] & 1
    mask = (0, 1 + side, 2 - side, 3)[near] + far
    return lax.shift_right_logical(id_ref[0], 1) ^ mask


def columns_of(width):
    return [slice(low, low + LANES) for low in range(0, width, LANES)]


def row_norms(block):
    rows, width = block.shape
    folded = None
    for cut in columns_of(width):
        part = block[:, cut].astype(jnp.float32)
        folded = part * part if folded is None else folded + part * part
    return jnp.sum(folded.T, axis=0, keepdims=True) * (1.0 / width)


def fill_scores(pieces, scale, id_ref, piece_refs, pool_ref, mask_ref, joined, out):
    own_rows = joined.shape[0] // len(pieces)
    low = 0
    for ref in piece_refs:
        joined[low : low + ref.shape[0], :] = ref[...]
        low += ref.shape[0]
    dots = lax.dot_general(
        joined[...],
        pool_ref[...],
        (((1,), (1,)), ((), ())),
        preferred_element_type=jnp.float32,
    )
    for k, piece in enumerate(pieces):
        rows = slice(k * own_rows, (k + 1) * own_rows)
        tile = lax.div(owner_of(id_ref, piece) * own_rows, TILE)
        out[rows, :] = dots[rows, :] * scale + mask_ref[pl.ds(tile, 1), :]


def diagonal(size):
    rows = lax.broadcasted_iota(jnp.int32, (size, size), 0)
    return rows == lax.broadcasted_iota(jnp.int32, (size, size), 1)


def row_pass(pieces, id_ref, shift, score_ref, held_ref):
    own_rows = held_ref.shape[1]
    eye = diagonal(own_rows)
    for k, piece in enumerate(pieces):
        block = score_ref[k * own_rows : (k + 1) * own_rows, :] + shift
        peak = jnp.max(block, axis=1, keepdims=True)
        total = jnp.sum(jnp.exp2(block - peak), axis=1, keepdims=True)
        sums = jnp.sum(jnp.where(eye, peak + log2(total), 0.0), axis=0, keepdims=True)
        held_ref[pl.ds(owner_of(id_ref, piece), 1), :] = sums


def copy_out(held_ref, out_ref):
    across = LANES // held_ref.shape[1]
    for line in range(out_ref.shape[1]):
        sources = [held_ref[line * across + k : line * across + k + 1, :] for k in range(across)]
        wide = jnp.concatenate(sources, axis=1)
        out_ref[:, line, :] = jnp.broadcast_to(wide, (out_ref.shape[0], LANES))


def prepare_kernel(list_hbm, count_hbm, own_ref, pool_ref, *refs):
    own_out, pool_out, own_norm_ref, pool_norm_ref, mask_ref = refs[:5]
    list_ref, count_ref, list_sem, count_sem, own_sem, pool_sem = refs[5:]
    list_copy = pltpu.make_async_copy(list_hbm, list_ref, list_sem)
    count_copy = pltpu.make_async_copy(count_hbm, count_ref, count_sem)
    list_copy.start()
    count_copy.start()
    own_copy = pltpu.make_async_copy(own_ref, own_out, own_sem)
    own_copy.start()
    pool_rows = pool_ref.shape[0]
    step = pool_rows // pool_sem.shape[0]
    copies = []
    for k in range(pool_sem.shape[0]):
        rows = pl.ds(k * step, step)
        copies.append(
            pltpu.make_async_copy(pool_ref.at[rows], pool_out.at[rows], pool_sem.at[k])
        )
        copies[-1].start()
    list_copy.wait()
    count_copy.wait()
    for t in range(mask_ref.shape[0]):
        for u in range(pool_rows // TILE):
            counted = jnp.int32(0)
            for k in range(CAP):
                hit = (list_ref[0, 0, 0, k] == t) & (list_ref[0, 0, 1, k] == u)
                counted += jnp.where(hit & (k < count_ref[0, 0]), 1, 0)
            offset = jnp.where(counted > 0, 0.0, NEG)
            mask_ref[t : t + 1, u * TILE : (u + 1) * TILE] = jnp.full((1, TILE), offset)
    own_copy.wait()
    own_norm_ref[...] = row_norms(own_out[...])
    for k, copy in enumerate(copies):
        copy.wait()
        for low in range(k * step, (k + 1) * step, LANES):
            rows = slice(low, low + LANES)
            pool_norm_ref[:, rows] = row_norms(pool_out[rows, :])


def early_kernel(pieces, scale, unit, id_ref, *refs):
    *piece_refs, pool_ref, norm_ref, mask_ref, score_ref, held_ref, joined = refs
    fill_scores(pieces, scale, id_ref, piece_refs, pool_ref, mask_ref, joined, score_ref)
    held_ref[...] = jnp.zeros_like(held_ref)
    row_pass(pieces, id_ref, norm_ref[...] * (-1.0 / unit), score_ref, held_ref)


def late_kernel(pieces, scale, unit, id_ref, *refs):
    *piece_refs, pool_ref, norm_ref, mask_ref, before_ref = refs[:-4]
    score_ref, out_ref, joined, held_ref = refs[-4:]
    fill_scores(pieces, scale, id_ref, piece_refs, pool_ref, mask_ref, joined, score_ref)
    held_ref[...] = before_ref[...]
    row_pass(pieces, id_ref, norm_ref[...] * (-1.0 / unit), score_ref, held_ref)
    copy_out(held_ref, out_ref)


def row_kernel(parts, id_ref, shift_ref, *refs):
    out_ref, held_ref = refs[-2:]
    shift = shift_ref[...]
    for ref, pieces in zip(refs[:-2], parts):
        row_pass(pieces, id_ref, shift, ref, held_ref)
    copy_out(held_ref, out_ref)


def column_kernel(parts, log_a, unit, id_ref, value_ref, norm_ref, *refs):
    scores, (out_ref, own_ref, held_ref) = refs[:-3], refs[-3:]
    shift = log_a - log2_sum([value_ref[k] for k in range(value_ref.shape[0])])
    size, own_rows = held_ref.shape
    pool_rows = out_ref.shape[1]
    across = LANES // own_rows
    for source in range(size):
        line, place = source // across, source % across
        held_ref[source : source + 1, :] = shift[
            line : line + 1, place * own_rows : (place + 1) * own_rows
        ]
    own = held_ref[pl.ds(owner_of(id_ref, (0, 0)), 1), :] * unit + norm_ref[...]
    own_ref[...] = jnp.broadcast_to(jnp.concatenate([own] * across, axis=1), own_ref.shape)
    eye = diagonal(own_rows)
    folded = (own_rows // SUBLANES, SUBLANES, pool_rows)
    blocks = [
        (ref, slice(k * own_rows, (k + 1) * own_rows), piece)
        for ref, pieces in zip(scores, parts)
        for k, piece in enumerate(pieces)
    ]
    columns = []
    peak = None
    for k, (ref, rows, piece) in enumerate(blocks):
        row = held_ref[pl.ds(owner_of(id_ref, piece), 1), :]
        columns.append(jnp.sum(jnp.where(eye, row, 0.0), axis=1, keepdims=True))
        high = jnp.max((ref[rows, :] + columns[k]).reshape(folded), axis=0)
        peak = high if peak is None else jnp.maximum(peak, high)
    peak = jnp.max(peak, axis=0, keepdims=True)
    total = jnp.zeros((SUBLANES, pool_rows), jnp.float32)
    for k, (ref, rows, _) in enumerate(blocks):
        total += jnp.sum(jnp.exp2(ref[rows, :] + (columns[k] - peak)).reshape(folded), axis=0)
    out_ref[...] = peak + log2(jnp.sum(total, axis=0, keepdims=True))


def call(kernel, shapes, scratch, scalars, arrays, flops, name):
    smem = pl.BlockSpec(memory_space=pltpu.SMEM)
    vmem = pl.BlockSpec(memory_space=pltpu.VMEM)
    moved = sum(a.size * a.dtype.itemsize for a in arrays) + 4 * sum(map(math.prod, shapes))
    return pl.pallas_call(
        kernel,
        out_shape=[jax.ShapeDtypeStruct(s, jnp.float32) for s in shapes],
        in_specs=[smem] * len(scalars) + [vmem] * len(arrays),
        out_specs=[vmem] * len(shapes),
        scratch_shapes=scratch,
        compiler_params=pltpu.CompilerParams(vmem_limit_bytes=3 * moved + (4 << 20)),
        cost_estimate=pl.CostEstimate(flops=flops, bytes_accessed=moved, transcendentals=0),
        name=name,
    )(*scalars, *arrays)


def prepare(tile_list, tile_count, own, pool, tiles):
    vmem = pl.BlockSpec(memory_space=pltpu.VMEM)
    chunks = 4
    shapes = [
        jax.ShapeDtypeStruct(own.shape, own.dtype),
        jax.ShapeDtypeStruct(pool.shape, pool.dtype),
        jax.ShapeDtypeStruct((1, own.shape[0]), jnp.float32),
        jax.ShapeDtypeStruct((1, pool.shape[0]), jnp.float32),
        jax.ShapeDtypeStruct((tiles, pool.shape[0]), jnp.float32),
    ]
    return pl.pallas_call(
        prepare_kernel,
        out_shape=shapes,
        in_specs=[pl.BlockSpec(memory_space=pltpu.HBM)] * 4,
        out_specs=[vmem] * len(shapes),
        scratch_shapes=[
            pltpu.SMEM(tile_list.shape, jnp.int32),
            pltpu.SMEM(tile_count.shape, jnp.int32),
            pltpu.SemaphoreType.DMA,
            pltpu.SemaphoreType.DMA,
            pltpu.SemaphoreType.DMA,
            pltpu.SemaphoreType.DMA((chunks,)),
        ],
        compiler_params=pltpu.CompilerParams(vmem_limit_bytes=16 << 20),
        cost_estimate=pl.CostEstimate(
            flops=2 * pool.size, bytes_accessed=4 * pool.size, transcendentals=0
        ),
        name="prepare",
    )(tile_list, tile_count, own, pool)


def body(samples, pool, tile_list, tile_count):
    own_rows, width = samples.shape[1:]
    size = lax.axis_size("pool")
    cores = lax.axis_size("samp")
    half_rows = own_rows * size
    pool_rows = pool.shape[0]
    lines = half_rows // LANES
    unit = EPS * LN2
    scale = 2.0 / (width * unit)
    log_a = -math.log2(half_rows * cores)
    log_b = -math.log2(pool_rows * size)
    own = samples.reshape(own_rows, width)

    def swap(value, masks):
        pairs = [
            (i * cores + c, (i ^ masks[c % 2]) * cores + c)
            for i in range(size)
            for c in range(cores)
        ]
        return lax.ppermute(value, ("pool", "samp"), pairs)

    def side_a(value):
        return swap(value, (1, 2))

    def side_b(value):
        return swap(value, (2, 1))

    def far(value, mask):
        return swap(value, (mask, mask))

    index = lax.axis_index("pool") * 2 + lax.axis_index("samp") % 2
    ids = [index.astype(jnp.int32).reshape(1)]

    far12, far4 = far(own, 12), far(own, 4)
    a, b = side_a(own), side_b(own)
    corner = swap(own, (3, 3))
    pairs = tile_list.swapaxes(2, 3)
    local = prepare(pairs, tile_count, own, pool, half_rows // TILE)
    far12, ids[0], *local = lax.optimization_barrier((far12, ids[0], *local))
    own_copy, pool_copy, own_norm, pool_norm, mask = local
    far8 = far(far12, 4)
    pair = jnp.concatenate([far4, far12], axis=0)
    a_pair, b_pair = side_a(pair), side_b(pair)
    a8, b8 = side_a(far8), side_b(far8)
    corner12, corner4 = far(corner, 12), far(corner, 4)
    corner8 = far(corner12, 4)
    early = [own_copy, a, b, corner, far4, far12, far8, a_pair, b_pair, b8]
    early_pieces = [(0, 0), (1, 0), (2, 0), (3, 0), (0, 4), (0, 12), (0, 8)]
    early_pieces += [(1, 4), (1, 12), (2, 4), (2, 12), (2, 8)]
    late = [a8, corner4, corner12, corner8]
    late_pieces = [(1, 8), (3, 4), (3, 12), (3, 8)]
    step = 16
    while step < size:
        late = late + [far(piece, step) for piece in early + late]
        late_pieces = late_pieces + [(near, z + step) for near, z in early_pieces + late_pieces]
        step *= 2

    count = len(early_pieces) * own_rows
    score0, held = call(
        functools.partial(early_kernel, early_pieces, scale, unit),
        [(count, pool_rows), (size, own_rows)],
        [pltpu.VMEM((count, width), samples.dtype)],
        ids,
        early + [pool_copy, pool_norm, mask],
        2 * count * pool_rows * width,
        "early_scores",
    )
    *late, score0, held = lax.optimization_barrier((*late, score0, held))
    count = len(late_pieces) * own_rows
    score1, value = call(
        functools.partial(late_kernel, late_pieces, scale, unit),
        [(count, pool_rows), (size, lines, LANES)],
        [
            pltpu.VMEM((count, width), samples.dtype),
            pltpu.VMEM((size, own_rows), jnp.float32),
        ],
        ids,
        late + [pool_copy, pool_norm, mask, held],
        2 * count * pool_rows * width,
        "late_scores",
    )
    parts = [early_pieces, late_pieces]
    scores = [score0, score1]
    flops = 8 * half_rows * pool_rows
    held = [pltpu.VMEM((size, own_rows), jnp.float32)]
    for iteration in range(ITERS):
        if iteration > 0:
            kernel = functools.partial(row_kernel, parts)
            shapes = [(size, lines, LANES)]
            (value,) = call(kernel, shapes, held, ids, [shift] + scores, flops, "rows")
        value = lax.all_to_all(value, "pool", 0, 0, tiled=True)
        value, sample_potential = call(
            functools.partial(column_kernel, parts, log_a, unit),
            [(1, pool_rows), (SUBLANES, LANES)],
            held,
            ids,
            [value, own_norm] + scores,
            flops,
            "columns",
        )
        pairs = [(i, i ^ 1) for i in range(cores)]
        shift = log_b - log2_sum([value, lax.ppermute(value, "samp", pairs)])
    return sample_potential[:1, :own_rows], (shift * unit + pool_norm).reshape(pool_rows)


def solution(mesh):
    placed = (
        P(("grp", "samp"), "pool", None),
        P(("grp", "pool"), None),
        P(("grp", "samp"), "pool", None, None),
        P(("grp", "samp"), "pool"),
    )
    return jax.shard_map(
        body,
        mesh=mesh,
        in_specs=placed,
        out_specs=(P(("grp", "samp"), "pool"), P(("grp", "pool"))),
        check_vma=False,
    )
```

```python
import functools
import math

import jax
import jax.numpy as jnp
from jax import lax
from jax.experimental import pallas as pl
from jax.experimental.pallas import tpu as pltpu
from jax.sharding import PartitionSpec as P

TILE = 512
CAP = 4
ITERS = 3


EPS = 0.02
NEG = -1e30
LN2 = math.log(2.0)
LANES = 128
SUBLANES = 8


def log2(value):
    return jnp.log(value) * (1.0 / LN2)


def log2_sum(values):
    peak = functools.reduce(jnp.maximum, values)
    total = functools.reduce(jnp.add, [jnp.exp2(v - peak) for v in values])
    return peak + log2(total)


def owner_of(id_ref, piece):
    near, far = piece
    side = id_ref[0] & 1
    mask = (0, 1 + side, 2 - side, 3)[near] + far
    return lax.shift_right_logical(id_ref[0], 1) ^ mask


def columns_of(width):
    return [slice(low, low + LANES) for low in range(0, width, LANES)]


def row_norms(block):
    rows, width = block.shape
    folded = None
    for cut in columns_of(width):
        part = block[:, cut].astype(jnp.float32)
        folded = part * part if folded is None else folded + part * part
    return jnp.sum(folded.T, axis=0, keepdims=True) * (1.0 / width)


def fill_scores(pieces, scale, id_ref, piece_refs, pool_ref, mask_ref, joined, out):
    own_rows = joined.shape[0] // len(pieces)
    low = 0
    for ref in piece_refs:
        joined[low : low + ref.shape[0], :] = ref[...]
        low += ref.shape[0]
    dots = lax.dot_general(
        joined[...],
        pool_ref[...],
        (((1,), (1,)), ((), ())),
        preferred_element_type=jnp.float32,
    )
    for k, piece in enumerate(pieces):
        rows = slice(k * own_rows, (k + 1) * own_rows)
        tile = lax.div(owner_of(id_ref, piece) * own_rows, TILE)
        out[rows, :] = dots[rows, :] * scale + mask_ref[pl.ds(tile, 1), :]


def diagonal(size):
    rows = lax.broadcasted_iota(jnp.int32, (size, size), 0)
    return rows == lax.broadcasted_iota(jnp.int32, (size, size), 1)


def row_pass(pieces, id_ref, shift, score_ref, held_ref):
    own_rows = held_ref.shape[1]
    eye = diagonal(own_rows)
    for k, piece in enumerate(pieces):
        block = score_ref[k * own_rows : (k + 1) * own_rows, :] + shift
        peak = jnp.max(block, axis=1, keepdims=True)
        total = jnp.sum(jnp.exp2(block - peak), axis=1, keepdims=True)
        sums = jnp.sum(jnp.where(eye, peak + log2(total), 0.0), axis=0, keepdims=True)
        held_ref[pl.ds(owner_of(id_ref, piece), 1), :] = sums


def copy_out(held_ref, out_ref):
    across = LANES // held_ref.shape[1]
    for line in range(out_ref.shape[1]):
        sources = [held_ref[line * across + k : line * across + k + 1, :] for k in range(across)]
        wide = jnp.concatenate(sources, axis=1)
        out_ref[:, line, :] = jnp.broadcast_to(wide, (out_ref.shape[0], LANES))


def prepare_kernel(list_hbm, count_hbm, pool_ref, *refs):
    pool_out, pool_norm_ref, mask_ref = refs[:3]
    list_ref, count_ref, list_sem, count_sem, pool_sem = refs[3:]
    list_copy = pltpu.make_async_copy(list_hbm, list_ref, list_sem)
    count_copy = pltpu.make_async_copy(count_hbm, count_ref, count_sem)
    list_copy.start()
    count_copy.start()
    pool_rows = pool_ref.shape[0]
    step = pool_rows // pool_sem.shape[0]
    copies = []
    for k in range(pool_sem.shape[0]):
        rows = pl.ds(k * step, step)
        copies.append(
            pltpu.make_async_copy(pool_ref.at[rows], pool_out.at[rows], pool_sem.at[k])
        )
        copies[-1].start()
    list_copy.wait()
    count_copy.wait()
    for t in range(mask_ref.shape[0]):
        for u in range(pool_rows // TILE):
            counted = jnp.int32(0)
            for k in range(CAP):
                hit = (list_ref[0, 0, 0, k] == t) & (list_ref[0, 0, 1, k] == u)
                counted += jnp.where(hit & (k < count_ref[0, 0]), 1, 0)
            offset = jnp.where(counted > 0, 0.0, NEG)
            mask_ref[t : t + 1, u * TILE : (u + 1) * TILE] = jnp.full((1, TILE), offset)
    for k, copy in enumerate(copies):
        copy.wait()
        for low in range(k * step, (k + 1) * step, LANES):
            rows = slice(low, low + LANES)
            pool_norm_ref[:, rows] = row_norms(pool_out[rows, :])


def early_kernel(pieces, scale, unit, id_ref, *refs):
    *piece_refs, pool_ref, norm_ref, mask_ref = refs[:-4]
    score_ref, held_ref, own_norm_ref, joined = refs[-4:]
    own_norm_ref[...] = jnp.zeros_like(own_norm_ref)
    own_norm_ref[:1, : held_ref.shape[1]] = row_norms(piece_refs[0][...])
    fill_scores(pieces, scale, id_ref, piece_refs, pool_ref, mask_ref, joined, score_ref)
    held_ref[...] = jnp.zeros_like(held_ref)
    row_pass(pieces, id_ref, norm_ref[...] * (-1.0 / unit), score_ref, held_ref)


def late_kernel(pieces, scale, unit, id_ref, *refs):
    *piece_refs, pool_ref, norm_ref, mask_ref, before_ref = refs[:-4]
    score_ref, out_ref, joined, held_ref = refs[-4:]
    fill_scores(pieces, scale, id_ref, piece_refs, pool_ref, mask_ref, joined, score_ref)
    held_ref[...] = before_ref[...]
    row_pass(pieces, id_ref, norm_ref[...] * (-1.0 / unit), score_ref, held_ref)
    copy_out(held_ref, out_ref)


def row_kernel(parts, id_ref, shift_ref, *refs):
    out_ref, held_ref = refs[-2:]
    shift = shift_ref[...]
    for ref, pieces in zip(refs[:-2], parts):
        row_pass(pieces, id_ref, shift, ref, held_ref)
    copy_out(held_ref, out_ref)


def column_kernel(parts, log_a, unit, id_ref, value_ref, norm_ref, *refs):
    scores, (out_ref, own_ref, held_ref) = refs[:-3], refs[-3:]
    shift = log_a - log2_sum([value_ref[k] for k in range(value_ref.shape[0])])
    size, own_rows = held_ref.shape
    pool_rows = out_ref.shape[1]
    across = LANES // own_rows
    for source in range(size):
        line, place = source // across, source % across
        held_ref[source : source + 1, :] = shift[
            line : line + 1, place * own_rows : (place + 1) * own_rows
        ]
    own = held_ref[pl.ds(owner_of(id_ref, (0, 0)), 1), :] * unit
    own += norm_ref[:1, :own_rows]
    own_ref[...] = jnp.broadcast_to(jnp.concatenate([own] * across, axis=1), own_ref.shape)
    eye = diagonal(own_rows)
    folded = (own_rows // SUBLANES, SUBLANES, pool_rows)
    blocks = [
        (ref, slice(k * own_rows, (k + 1) * own_rows), piece)
        for ref, pieces in zip(scores, parts)
        for k, piece in enumerate(pieces)
    ]
    columns = []
    peak = None
    for k, (ref, rows, piece) in enumerate(blocks):
        row = held_ref[pl.ds(owner_of(id_ref, piece), 1), :]
        columns.append(jnp.sum(jnp.where(eye, row, 0.0), axis=1, keepdims=True))
        high = jnp.max((ref[rows, :] + columns[k]).reshape(folded), axis=0)
        peak = high if peak is None else jnp.maximum(peak, high)
    peak = jnp.max(peak, axis=0, keepdims=True)
    total = jnp.zeros((SUBLANES, pool_rows), jnp.float32)
    for k, (ref, rows, _) in enumerate(blocks):
        total += jnp.sum(jnp.exp2(ref[rows, :] + (columns[k] - peak)).reshape(folded), axis=0)
    out_ref[...] = peak + log2(jnp.sum(total, axis=0, keepdims=True))


def call(kernel, shapes, scratch, scalars, arrays, flops, name):
    smem = pl.BlockSpec(memory_space=pltpu.SMEM)
    vmem = pl.BlockSpec(memory_space=pltpu.VMEM)
    moved = sum(a.size * a.dtype.itemsize for a in arrays) + 4 * sum(map(math.prod, shapes))
    return pl.pallas_call(
        kernel,
        out_shape=[jax.ShapeDtypeStruct(s, jnp.float32) for s in shapes],
        in_specs=[smem] * len(scalars) + [vmem] * len(arrays),
        out_specs=[vmem] * len(shapes),
        scratch_shapes=scratch,
        compiler_params=pltpu.CompilerParams(vmem_limit_bytes=3 * moved + (4 << 20)),
        cost_estimate=pl.CostEstimate(flops=flops, bytes_accessed=moved, transcendentals=0),
        name=name,
    )(*scalars, *arrays)


def prepare(tile_list, tile_count, pool, tiles):
    vmem = pl.BlockSpec(memory_space=pltpu.VMEM)
    chunks = 4
    shapes = [
        jax.ShapeDtypeStruct(pool.shape, pool.dtype),
        jax.ShapeDtypeStruct((1, pool.shape[0]), jnp.float32),
        jax.ShapeDtypeStruct((tiles, pool.shape[0]), jnp.float32),
    ]
    return pl.pallas_call(
        prepare_kernel,
        out_shape=shapes,
        in_specs=[pl.BlockSpec(memory_space=pltpu.HBM)] * 3,
        out_specs=[vmem] * len(shapes),
        scratch_shapes=[
            pltpu.SMEM(tile_list.shape, jnp.int32),
            pltpu.SMEM(tile_count.shape, jnp.int32),
            pltpu.SemaphoreType.DMA,
            pltpu.SemaphoreType.DMA,
            pltpu.SemaphoreType.DMA((chunks,)),
        ],
        compiler_params=pltpu.CompilerParams(vmem_limit_bytes=16 << 20),
        cost_estimate=pl.CostEstimate(
            flops=2 * pool.size, bytes_accessed=4 * pool.size, transcendentals=0
        ),
        name="prepare",
    )(tile_list, tile_count, pool)


def body(samples, pool, tile_list, tile_count):
    own_rows, width = samples.shape[1:]
    size = lax.axis_size("pool")
    cores = lax.axis_size("samp")
    half_rows = own_rows * size
    pool_rows = pool.shape[0]
    lines = half_rows // LANES
    unit = EPS * LN2
    scale = 2.0 / (width * unit)
    log_a = -math.log2(half_rows * cores)
    log_b = -math.log2(pool_rows * size)
    own = samples.reshape(own_rows, width)

    def swap(value, masks):
        pairs = [
            (i * cores + c, (i ^ masks[c % 2]) * cores + c)
            for i in range(size)
            for c in range(cores)
        ]
        return lax.ppermute(value, ("pool", "samp"), pairs)

    def side_a(value):
        return swap(value, (1, 2))

    def side_b(value):
        return swap(value, (2, 1))

    def far(value, mask):
        return swap(value, (mask, mask))

    index = lax.axis_index("pool") * 2 | (lax.axis_index("samp") & 1)
    ids = [index.astype(jnp.int32).reshape(1)]

    far12, far4 = far(own, 12), far(own, 4)
    a, b = side_a(own), side_b(own)
    corner = swap(own, (3, 3))
    pairs = tile_list.swapaxes(2, 3)
    local = prepare(pairs, tile_count, pool, half_rows // TILE)
    far12, ids[0], *local = lax.optimization_barrier((far12, ids[0], *local))
    pool_copy, pool_norm, mask = local
    far8 = far(far12, 4)
    pair = jnp.concatenate([far4, far12], axis=0)
    a_pair, b_pair = side_a(pair), side_b(pair)
    a8, b8 = side_a(far8), side_b(far8)
    corner12, corner4 = far(corner, 12), far(corner, 4)
    corner8 = far(corner12, 4)
    early = [own, a, b, corner, far4, far12, far8, a_pair, b_pair, b8]
    early_pieces = [(0, 0), (1, 0), (2, 0), (3, 0), (0, 4), (0, 12), (0, 8)]
    early_pieces += [(1, 4), (1, 12), (2, 4), (2, 12), (2, 8)]
    late = [a8, corner4, corner12, corner8]
    late_pieces = [(1, 8), (3, 4), (3, 12), (3, 8)]
    step = 16
    while step < size:
        late = late + [far(piece, step) for piece in early + late]
        late_pieces = late_pieces + [(near, z + step) for near, z in early_pieces + late_pieces]
        step *= 2

    count = len(early_pieces) * own_rows
    score0, held, own_norm = call(
        functools.partial(early_kernel, early_pieces, scale, unit),
        [(count, pool_rows), (size, own_rows), (SUBLANES, LANES)],
        [pltpu.VMEM((count, width), samples.dtype)],
        ids,
        early + [pool_copy, pool_norm, mask],
        2 * count * pool_rows * width,
        "early_scores",
    )
    *late, score0, held, own_norm = lax.optimization_barrier((*late, score0, held, own_norm))
    count = len(late_pieces) * own_rows
    score1, value = call(
        functools.partial(late_kernel, late_pieces, scale, unit),
        [(count, pool_rows), (size, lines, LANES)],
        [
            pltpu.VMEM((count, width), samples.dtype),
            pltpu.VMEM((size, own_rows), jnp.float32),
        ],
        ids,
        late + [pool_copy, pool_norm, mask, held],
        2 * count * pool_rows * width,
        "late_scores",
    )
    parts = [early_pieces, late_pieces]
    scores = [score0, score1]
    flops = 8 * half_rows * pool_rows
    held = [pltpu.VMEM((size, own_rows), jnp.float32)]
    for iteration in range(ITERS):
        if iteration > 0:
            kernel = functools.partial(row_kernel, parts)
            shapes = [(size, lines, LANES)]
            (value,) = call(kernel, shapes, held, ids, [shift] + scores, flops, "rows")
        value = lax.all_to_all(value, "pool", 0, 0, tiled=True)
        value, sample_potential = call(
            functools.partial(column_kernel, parts, log_a, unit),
            [(1, pool_rows), (SUBLANES, LANES)],
            held,
            ids,
            [value, own_norm] + scores,
            flops,
            "columns",
        )
        pairs = [(i, i ^ 1) for i in range(cores)]
        shift = log_b - log2_sum([value, lax.ppermute(value, "samp", pairs)])
    return sample_potential[:1, :own_rows], (shift * unit + pool_norm).reshape(pool_rows)


def solution(mesh):
    placed = (
        P(("grp", "samp"), "pool", None),
        P(("grp", "pool"), None),
        P(("grp", "samp"), "pool", None, None),
        P(("grp", "samp"), "pool"),
    )
    return jax.shard_map(
        body,
        mesh=mesh,
        in_specs=placed,
        out_specs=(P(("grp", "samp"), "pool"), P(("grp", "pool"))),
        check_vma=False,
    )
```

```python
import functools
import math

import jax
import jax.numpy as jnp
from jax import lax
from jax.experimental import pallas as pl
from jax.experimental.pallas import tpu as pltpu
from jax.sharding import PartitionSpec as P

TILE = 512
CAP = 4
ITERS = 3


EPS = 0.02
NEG = -1e30
LN2 = math.log(2.0)
LANES = 128
SUBLANES = 8


def log2(value):
    return jnp.log(value) * (1.0 / LN2)


def log2_sum(values):
    peak = functools.reduce(jnp.maximum, values)
    total = functools.reduce(jnp.add, [jnp.exp2(v - peak) for v in values])
    return peak + log2(total)


def owner_of(id_ref, piece):
    near, far = piece
    side = id_ref[0] & 1
    mask = (0, 1 + side, 2 - side, 3)[near] + far
    return lax.shift_right_logical(id_ref[0], 1) ^ mask


def columns_of(width):
    return [slice(low, low + LANES) for low in range(0, width, LANES)]


def row_norms(block):
    rows, width = block.shape
    folded = None
    for cut in columns_of(width):
        part = block[:, cut].astype(jnp.float32)
        folded = part * part if folded is None else folded + part * part
    return jnp.sum(folded.T, axis=0, keepdims=True) * (1.0 / width)


def fill_scores(pieces, scale, id_ref, piece_refs, pool_ref, mask_ref, joined, out):
    own_rows = joined.shape[0] // len(pieces)
    low = 0
    for ref in piece_refs:
        joined[low : low + ref.shape[0], :] = ref[...]
        low += ref.shape[0]
    dots = lax.dot_general(
        joined[...],
        pool_ref[...],
        (((1,), (1,)), ((), ())),
        preferred_element_type=jnp.float32,
    )
    for k, piece in enumerate(pieces):
        rows = slice(k * own_rows, (k + 1) * own_rows)
        tile = lax.div(owner_of(id_ref, piece) * own_rows, TILE)
        out[rows, :] = dots[rows, :] * scale + mask_ref[pl.ds(tile, 1), :]


def diagonal(size):
    rows = lax.broadcasted_iota(jnp.int32, (size, size), 0)
    return rows == lax.broadcasted_iota(jnp.int32, (size, size), 1)


def row_pass(pieces, id_ref, shift, score_ref, held_ref):
    own_rows = held_ref.shape[1]
    eye = diagonal(own_rows)
    for k, piece in enumerate(pieces):
        block = score_ref[k * own_rows : (k + 1) * own_rows, :] + shift
        peak = jnp.max(block, axis=1, keepdims=True)
        total = jnp.sum(jnp.exp2(block - peak), axis=1, keepdims=True)
        sums = jnp.sum(jnp.where(eye, peak + log2(total), 0.0), axis=0, keepdims=True)
        held_ref[pl.ds(owner_of(id_ref, piece), 1), :] = sums


def copy_out(held_ref, out_ref):
    across = LANES // held_ref.shape[1]
    for line in range(out_ref.shape[1]):
        sources = [held_ref[line * across + k : line * across + k + 1, :] for k in range(across)]
        wide = jnp.concatenate(sources, axis=1)
        out_ref[:, line, :] = jnp.broadcast_to(wide, (out_ref.shape[0], LANES))


def prepare_kernel(list_hbm, count_hbm, pool_ref, *refs):
    pool_out, pool_norm_ref, mask_ref = refs[:3]
    list_ref, count_ref, list_sem, count_sem, pool_sem = refs[3:]
    list_copy = pltpu.make_async_copy(list_hbm, list_ref, list_sem)
    count_copy = pltpu.make_async_copy(count_hbm, count_ref, count_sem)
    list_copy.start()
    count_copy.start()
    pool_rows = pool_ref.shape[0]
    step = pool_rows // pool_sem.shape[0]
    copies = []
    for k in range(pool_sem.shape[0]):
        rows = pl.ds(k * step, step)
        copies.append(
            pltpu.make_async_copy(pool_ref.at[rows], pool_out.at[rows], pool_sem.at[k])
        )
        copies[-1].start()
    list_copy.wait()
    count_copy.wait()
    for t in range(mask_ref.shape[0]):
        for u in range(pool_rows // TILE):
            counted = jnp.int32(0)
            for k in range(CAP):
                hit = (list_ref[0, 0, 0, k] == t) & (list_ref[0, 0, 1, k] == u)
                counted += jnp.where(hit & (k < count_ref[0, 0]), 1, 0)
            offset = jnp.where(counted > 0, 0.0, NEG)
            mask_ref[t : t + 1, u * TILE : (u + 1) * TILE] = jnp.full((1, TILE), offset)
    for k, copy in enumerate(copies):
        copy.wait()
        for low in range(k * step, (k + 1) * step, LANES):
            rows = slice(low, low + LANES)
            pool_norm_ref[:, rows] = row_norms(pool_out[rows, :])


def early_kernel(pieces, scale, unit, id_ref, *refs):
    *piece_refs, pool_ref, norm_ref, mask_ref = refs[:-4]
    score_ref, held_ref, own_norm_ref, joined = refs[-4:]
    own_norm_ref[...] = jnp.zeros_like(own_norm_ref)
    own_norm_ref[:1, : held_ref.shape[1]] = row_norms(piece_refs[0][...])
    fill_scores(pieces, scale, id_ref, piece_refs, pool_ref, mask_ref, joined, score_ref)
    held_ref[...] = jnp.zeros_like(held_ref)
    row_pass(pieces, id_ref, norm_ref[...] * (-1.0 / unit), score_ref, held_ref)


def late_kernel(pieces, scale, unit, id_ref, *refs):
    *piece_refs, pool_ref, norm_ref, mask_ref, before_ref = refs[:-4]
    score_ref, out_ref, joined, held_ref = refs[-4:]
    fill_scores(pieces, scale, id_ref, piece_refs, pool_ref, mask_ref, joined, score_ref)
    held_ref[...] = before_ref[...]
    row_pass(pieces, id_ref, norm_ref[...] * (-1.0 / unit), score_ref, held_ref)
    copy_out(held_ref, out_ref)


def row_kernel(parts, id_ref, shift_ref, *refs):
    out_ref, held_ref = refs[-2:]
    shift = shift_ref[...]
    for ref, pieces in zip(refs[:-2], parts):
        row_pass(pieces, id_ref, shift, ref, held_ref)
    copy_out(held_ref, out_ref)


def column_kernel(parts, log_a, unit, id_ref, value_ref, norm_ref, *refs):
    scores, (out_ref, own_ref, held_ref) = refs[:-3], refs[-3:]
    shift = log_a - log2_sum([value_ref[k] for k in range(value_ref.shape[0])])
    size, own_rows = held_ref.shape
    pool_rows = out_ref.shape[1]
    across = LANES // own_rows
    for source in range(size):
        line, place = source // across, source % across
        held_ref[source : source + 1, :] = shift[
            line : line + 1, place * own_rows : (place + 1) * own_rows
        ]
    own = held_ref[pl.ds(owner_of(id_ref, (0, 0)), 1), :] * unit
    own += norm_ref[:1, :own_rows]
    own_ref[...] = jnp.broadcast_to(jnp.concatenate([own] * across, axis=1), own_ref.shape)
    eye = diagonal(own_rows)
    folded = (own_rows // SUBLANES, SUBLANES, pool_rows)
    blocks = [
        (ref, slice(k * own_rows, (k + 1) * own_rows), piece)
        for ref, pieces in zip(scores, parts)
        for k, piece in enumerate(pieces)
    ]
    columns = []
    peak = None
    for k, (ref, rows, piece) in enumerate(blocks):
        row = held_ref[pl.ds(owner_of(id_ref, piece), 1), :]
        columns.append(jnp.sum(jnp.where(eye, row, 0.0), axis=1, keepdims=True))
        high = jnp.max((ref[rows, :] + columns[k]).reshape(folded), axis=0)
        peak = high if peak is None else jnp.maximum(peak, high)
    total = jnp.zeros((SUBLANES, pool_rows), jnp.float32)
    for k, (ref, rows, _) in enumerate(blocks):
        block = (ref[rows, :] + columns[k]).reshape(folded)
        total += jnp.sum(jnp.exp2(block - peak), axis=0)
    top = jnp.max(peak, axis=0, keepdims=True)
    total = jnp.sum(total * jnp.exp2(peak - top), axis=0, keepdims=True)
    out_ref[...] = top + log2(total)


def call(kernel, shapes, scratch, scalars, arrays, flops, name):
    smem = pl.BlockSpec(memory_space=pltpu.SMEM)
    vmem = pl.BlockSpec(memory_space=pltpu.VMEM)
    moved = sum(a.size * a.dtype.itemsize for a in arrays) + 4 * sum(map(math.prod, shapes))
    return pl.pallas_call(
        kernel,
        out_shape=[jax.ShapeDtypeStruct(s, jnp.float32) for s in shapes],
        in_specs=[smem] * len(scalars) + [vmem] * len(arrays),
        out_specs=[vmem] * len(shapes),
        scratch_shapes=scratch,
        compiler_params=pltpu.CompilerParams(vmem_limit_bytes=3 * moved + (4 << 20)),
        cost_estimate=pl.CostEstimate(flops=flops, bytes_accessed=moved, transcendentals=0),
        name=name,
    )(*scalars, *arrays)


def prepare(tile_list, tile_count, pool, tiles):
    vmem = pl.BlockSpec(memory_space=pltpu.VMEM)
    chunks = 4
    shapes = [
        jax.ShapeDtypeStruct(pool.shape, pool.dtype),
        jax.ShapeDtypeStruct((1, pool.shape[0]), jnp.float32),
        jax.ShapeDtypeStruct((tiles, pool.shape[0]), jnp.float32),
    ]
    return pl.pallas_call(
        prepare_kernel,
        out_shape=shapes,
        in_specs=[pl.BlockSpec(memory_space=pltpu.HBM)] * 3,
        out_specs=[vmem] * len(shapes),
        scratch_shapes=[
            pltpu.SMEM(tile_list.shape, jnp.int32),
            pltpu.SMEM(tile_count.shape, jnp.int32),
            pltpu.SemaphoreType.DMA,
            pltpu.SemaphoreType.DMA,
            pltpu.SemaphoreType.DMA((chunks,)),
        ],
        compiler_params=pltpu.CompilerParams(vmem_limit_bytes=16 << 20),
        cost_estimate=pl.CostEstimate(
            flops=2 * pool.size, bytes_accessed=4 * pool.size, transcendentals=0
        ),
        name="prepare",
    )(tile_list, tile_count, pool)


def body(samples, pool, tile_list, tile_count):
    own_rows, width = samples.shape[1:]
    size = lax.axis_size("pool")
    cores = lax.axis_size("samp")
    half_rows = own_rows * size
    pool_rows = pool.shape[0]
    lines = half_rows // LANES
    unit = EPS * LN2
    scale = 2.0 / (width * unit)
    log_a = -math.log2(half_rows * cores)
    log_b = -math.log2(pool_rows * size)
    own = samples.reshape(own_rows, width)

    def swap(value, masks):
        pairs = [
            (i * cores + c, (i ^ masks[c % 2]) * cores + c)
            for i in range(size)
            for c in range(cores)
        ]
        return lax.ppermute(value, ("pool", "samp"), pairs)

    def side_a(value):
        return swap(value, (1, 2))

    def side_b(value):
        return swap(value, (2, 1))

    def far(value, mask):
        return swap(value, (mask, mask))

    index = lax.axis_index("pool") * 2 | (lax.axis_index("samp") & 1)
    ids = [index.astype(jnp.int32).reshape(1)]

    far12, far4 = far(own, 12), far(own, 4)
    a, b = side_a(own), side_b(own)
    corner = swap(own, (3, 3))
    pairs = tile_list.swapaxes(2, 3)
    local = prepare(pairs, tile_count, pool, half_rows // TILE)
    far12, far4, ids[0], *local = lax.optimization_barrier((far12, far4, ids[0], *local))
    pool_copy, pool_norm, mask = local
    far8 = far(far12, 4)
    far4, corner = lax.optimization_barrier((far4, corner))
    pair = jnp.concatenate([far4, far12], axis=0)
    a_pair, b_pair = side_a(pair), side_b(pair)
    a8, b8 = side_a(far8), side_b(far8)
    corner12, corner4 = far(corner, 12), far(corner, 4)
    corner8 = far(corner12, 4)
    early = [own, a, b, corner, far4, far12, far8, a_pair, b_pair, b8]
    early_pieces = [(0, 0), (1, 0), (2, 0), (3, 0), (0, 4), (0, 12), (0, 8)]
    early_pieces += [(1, 4), (1, 12), (2, 4), (2, 12), (2, 8)]
    late = [a8, corner4, corner12, corner8]
    late_pieces = [(1, 8), (3, 4), (3, 12), (3, 8)]
    step = 16
    while step < size:
        late = late + [far(piece, step) for piece in early + late]
        late_pieces = late_pieces + [(near, z + step) for near, z in early_pieces + late_pieces]
        step *= 2

    count = len(early_pieces) * own_rows
    score0, held, own_norm = call(
        functools.partial(early_kernel, early_pieces, scale, unit),
        [(count, pool_rows), (size, own_rows), (SUBLANES, LANES)],
        [pltpu.VMEM((count, width), samples.dtype)],
        ids,
        early + [pool_copy, pool_norm, mask],
        2 * count * pool_rows * width,
        "early_scores",
    )
    *late, score0, held, own_norm = lax.optimization_barrier((*late, score0, held, own_norm))
    count = len(late_pieces) * own_rows
    score1, value = call(
        functools.partial(late_kernel, late_pieces, scale, unit),
        [(count, pool_rows), (size, lines, LANES)],
        [
            pltpu.VMEM((count, width), samples.dtype),
            pltpu.VMEM((size, own_rows), jnp.float32),
        ],
        ids,
        late + [pool_copy, pool_norm, mask, held],
        2 * count * pool_rows * width,
        "late_scores",
    )
    parts = [early_pieces, late_pieces]
    scores = [score0, score1]
    flops = 8 * half_rows * pool_rows
    held = [pltpu.VMEM((size, own_rows), jnp.float32)]
    for iteration in range(ITERS):
        if iteration > 0:
            kernel = functools.partial(row_kernel, parts)
            shapes = [(size, lines, LANES)]
            (value,) = call(kernel, shapes, held, ids, [shift] + scores, flops, "rows")
        value = lax.all_to_all(value, "pool", 0, 0, tiled=True)
        value, sample_potential = call(
            functools.partial(column_kernel, parts, log_a, unit),
            [(1, pool_rows), (SUBLANES, LANES)],
            held,
            ids,
            [value, own_norm] + scores,
            flops,
            "columns",
        )
        pairs = [(i, i ^ 1) for i in range(cores)]
        shift = log_b - log2_sum([value, lax.ppermute(value, "samp", pairs)])
    return sample_potential[:1, :own_rows], (shift * unit + pool_norm).reshape(pool_rows)


def solution(mesh):
    placed = (
        P(("grp", "samp"), "pool", None),
        P(("grp", "pool"), None),
        P(("grp", "samp"), "pool", None, None),
        P(("grp", "samp"), "pool"),
    )
    return jax.shard_map(
        body,
        mesh=mesh,
        in_specs=placed,
        out_specs=(P(("grp", "samp"), "pool"), P(("grp", "pool"))),
        check_vma=False,
    )
```
